32 devices in a mesh: client: 4 (over x, core), shard: 8 (over z, y).
Axes of the slice: x: 2, y: 2, z: 4, core: 2. Of those that a mesh axis runs over, the one named last changes fastest.
Arguments:
- token_ids: int32 [4, 8, 512], P('client', 'shard'), may hold values from 0 to 50303
- lengths: int32 [4, 8], P('client', 'shard'), may hold values from 1 to 512, as said below
- picked: int32 [4, 8, 128], P('client', 'shard'), may hold values from 0 to 510
- joining: int32 [4], replicated, may hold values from 0 to 1, as said below
- embedding: float32 [50304, 768], P(('client', 'shard')), may hold values from -0.4375 to 0.4375
- embedding_first: float32 [50304, 768], P(('client', 'shard')), may hold values from -1.5258789e-05 to 1.5258789e-05
- embedding_second: float32 [50304, 768], P(('client', 'shard')), may hold values from 6.679406e-13 to 1.0687049e-11
- position_table: float32 [1024, 768], P(('client', 'shard')), may hold values from -0.75 to 0.75
- position_first: float32 [1024, 768], P(('client', 'shard')), may hold values from -1.5258789e-05 to 1.5258789e-05
- position_second: float32 [1024, 768], P(('client', 'shard')), may hold values from 6.679406e-13 to 1.0687049e-11
- shared_wide: float32 [768, 6144], P(('client', 'shard')), may hold values from -0.21875 to 0.21875
- shared_wide_first: float32 [768, 6144], P(('client', 'shard')), may hold values from -1.5258789e-05 to 1.5258789e-05
- shared_wide_second: float32 [768, 6144], P(('client', 'shard')), may hold values from 6.679406e-13 to 1.0687049e-11
- shared_down: float32 [3072, 768], P(('client', 'shard')), may hold values from -0.109375 to 0.109375
- shared_down_first: float32 [3072, 768], P(('client', 'shard')), may hold values from -1.5258789e-05 to 1.5258789e-05
- shared_down_second: float32 [3072, 768], P(('client', 'shard')), may hold values from 6.679406e-13 to 1.0687049e-11
- shared_vectors: float32 [10752], P(('client', 'shard'))
- shared_vectors_first: float32 [10752], P(('client', 'shard')), may hold values from -6.1035156e-05 to 6.1035156e-05
- shared_vectors_second: float32 [10752], P(('client', 'shard')), may hold values from 1.0687049e-11 to 1.7099279e-10
- private_wide: float32 [4, 768, 6144], P('client', 'shard'), may hold values from -0.21875 to 0.21875
- private_wide_first: float32 [4, 768, 6144], P('client', 'shard'), may hold values from -1.5258789e-05 to 1.5258789e-05
- private_wide_second: float32 [4, 768, 6144], P('client', 'shard'), may hold values from 6.679406e-13 to 1.0687049e-11
- private_down: float32 [4, 3072, 768], P('client', 'shard'), may hold values from -0.109375 to 0.109375
- private_down_first: float32 [4, 3072, 768], P('client', 'shard'), may hold values from -1.5258789e-05 to 1.5258789e-05
- private_down_second: float32 [4, 3072, 768], P('client', 'shard'), may hold values from 6.679406e-13 to 1.0687049e-11
- private_vectors: float32 [4, 9216], P('client', 'shard')
- private_vectors_first: float32 [4, 9216], P('client', 'shard'), may hold values from -6.1035156e-05 to 6.1035156e-05
- private_vectors_second: float32 [4, 9216], P('client', 'shard'), may hold values from 1.0687049e-11 to 1.7099279e-10
Outputs:
- new_embedding: float32 [50304, 768], P(('client', 'shard'))
- new_embedding_first: float32 [50304, 768], P(('client', 'shard'))
- new_embedding_second: float32 [50304, 768], P(('client', 'shard'))
- new_position: float32 [1024, 768], P(('client', 'shard'))
- new_position_first: float32 [1024, 768], P(('client', 'shard'))
- new_position_second: float32 [1024, 768], P(('client', 'shard'))
- new_shared_wide: float32 [768, 6144], P(('client', 'shard'))
- new_shared_wide_first: float32 [768, 6144], P(('client', 'shard'))
- new_shared_wide_second: float32 [768, 6144], P(('client', 'shard'))
- new_shared_down: float32 [3072, 768], P(('client', 'shard'))
- new_shared_down_first: float32 [3072, 768], P(('client', 'shard'))
- new_shared_down_second: float32 [3072, 768], P(('client', 'shard'))
- new_shared_vectors: float32 [10752], P(('client', 'shard'))
- new_shared_vectors_first: float32 [10752], P(('client', 'shard'))
- new_shared_vectors_second: float32 [10752], P(('client', 'shard'))
- new_private_wide: float32 [4, 768, 6144], P('client', 'shard')
- new_private_wide_first: float32 [4, 768, 6144], P('client', 'shard')
- new_private_wide_second: float32 [4, 768, 6144], P('client', 'shard')
- new_private_down: float32 [4, 3072, 768], P('client', 'shard')
- new_private_down_first: float32 [4, 3072, 768], P('client', 'shard')
- new_private_down_second: float32 [4, 3072, 768], P('client', 'shard')
- new_private_vectors: float32 [4, 9216], P('client', 'shard')
- new_private_vectors_first: float32 [4, 9216], P('client', 'shard')
- new_private_vectors_second: float32 [4, 9216], P('client', 'shard')
- client_sums: float32 [4], P('client')
- client_counts: float32 [4], P('client')
- grad_norm: float32 [], replicated
The draws below stay inside these ranges and needn't reach their ends.
Inputs may be any that keep to these rules, and one draw needn't show every extreme that they name: `lengths`: in every client some sequence has all 512 slots live. `joining`: at least two clients take part and at least one does not.
All inputs are finite; a program needn't handle non-finite values.
Results may differ from the reference program's by a relative error of at most 0.018.
Values may be sent and summed in bfloat16 or wider, within the bound.
No kernel may reach another device: no remote copies, remote signals or barrier semaphores. Data moves between devices by JAX's collectives and lax.ppermute only.
A program may use at most 448 MiB of HBM per device.

```python
import math
import jax
import jax.numpy as jnp
import numpy as np
from jax import lax

HD = 64
D = 768
FF = 3072
VOCAB = 50304
NPOS = 1024
LEN = 512
PICK = 128
STEP = 5
CLIENTS = 4
SEQS = 8
PARAMS = 74856960


def vector_draw(key, total, gain_starts, breadth, leading):
    normal_draw = jnp.clip(jax.random.normal(key, leading + (total,), jnp.float32), -4.0, 4.0)
    index = jnp.arange(total)
    is_gain = index < 0
    for begin in gain_starts:
        is_gain = is_gain | (index >= begin) & (index < begin + breadth)
    return jnp.where(is_gain, 1.0 + 0.15 * normal_draw, 0.2 * normal_draw)


def draw_shared_vectors(key, part):
    key = jax.random.fold_in(key, 3)
    return vector_draw(key, 10 * D + FF, [0, 5 * D, 8 * D + FF], D, ())


def draw_private_vectors(key, part):
    key = jax.random.fold_in(key, 4)
    return vector_draw(key, 8 * D + FF, [0, 5 * D], D, (CLIENTS,))


def draw_lengths(key, part):
    key = jax.random.fold_in(key, 1)
    index = jnp.arange(SEQS, dtype=jnp.int32)
    upper = LEN // 3 + (LEN - LEN // 3) * (index + 1) // SEQS
    cut_off = jax.random.randint(key, (CLIENTS, SEQS), 0, 1 << 20) % (upper // 4 + 1)
    values = upper[None, :] - cut_off
    values = jnp.where(index[None, :] == SEQS - 1, LEN, values)
    return values.astype(jnp.int32)


def draw_joining(key, part):
    key = jax.random.fold_in(key, 2)
    first_key, second_key = jax.random.split(key)
    chosen = jax.random.randint(first_key, (), 2, CLIENTS)
    order = jax.random.permutation(second_key, CLIENTS)
    return (order < chosen).astype(jnp.int32)


def place_ends(array, stream_key, least, largest):
    longest = array.shape.index(max(array.shape))
    spots = []
    for shift in (0, 1):
        where = [jax.random.randint(jax.random.fold_in(stream_key, axis), (), 0, length) for axis, length in enumerate(array.shape)]
        where[longest] = (where[longest] + shift) % array.shape[longest]
        spots.append(tuple(where))
    return array.at[spots[0]].set(least).at[spots[1]].set(largest)


def levels(rng, extent, cuts, low, top_value):
    gain, own = 1.0, jax.random.fold_in(rng, 6)
    for axis_at, blocks in cuts:
        draws = jnp.exp(jax.random.uniform(jax.random.fold_in(own, axis_at), (blocks,), jnp.float32, low / len(cuts), top_value / len(cuts)))
        gain = gain * jnp.repeat(draws, extent[axis_at] // blocks).reshape([-1 if axis == axis_at else 1 for axis in range(len(extent))])
    return gain


def cumulative_ranks(number_of, lean):
    portions = [(1 << 20) // math.isqrt(standing ** lean) + 1 for standing in range(1, number_of + 1)]
    scale = 1 + sum(portions) // (1 << 30)
    return np.cumsum(np.array([max(1, weight // scale) for weight in portions]))


def ranked(key, dims, count, lean):
    grid = cumulative_ranks(count, lean)
    lot = jax.random.randint(jax.random.fold_in(key, 1), dims, 0, int(grid[count - 1]))
    grade = jnp.searchsorted(jnp.asarray(grid, jnp.int32), lot, side="right")
    return jax.random.permutation(jax.random.fold_in(key, 2), count)[grade].astype(jnp.int32)


def bell_draw(own_key, extent, scale, bound, cuts=(), held_as=jnp.bfloat16):
    factor_of = levels(own_key, extent, cuts, -0.22, 0.18) if cuts else 1.0
    values = jax.random.normal(own_key, extent, jnp.float32) * scale * factor_of
    return jnp.minimum(jnp.maximum(values, -bound), bound).astype(held_as)


def setup_inputs(seed: int = 0) -> dict:
    seeds = jax.random.split(jax.random.key(seed), 29)
    return {
        "token_ids": place_ends(ranked(seeds[0], (CLIENTS, SEQS, LEN), VOCAB, 2), jax.random.fold_in(seeds[0], 3), 0, VOCAB - 1).astype(jnp.int32),
        "lengths": draw_lengths(jax.random.fold_in(seeds[28], 71), 0),
        "picked": place_ends(jax.random.randint(seeds[2], (CLIENTS, SEQS, PICK), 0, LEN - 1), jax.random.fold_in(seeds[2], 1), 0, (LEN - 1) - 1).astype(jnp.int32),
        "joining": draw_joining(jax.random.fold_in(seeds[28], 71), 0),
        "embedding": bell_draw(seeds[4], (VOCAB, D), (D // 4) ** -0.5, 0.4375, ((0, 32),), jnp.float32),
        "embedding_first": bell_draw(seeds[5], (VOCAB, D), (0.01 / PARAMS ** 0.5), 1.52587890625e-05, ((0, 32),), jnp.float32),
        "embedding_second": jnp.clip(jnp.exp(math.log(1.0687049335766918e-11) - 2.7725887 * jax.random.uniform(seeds[6], (VOCAB, D), jnp.float32) ** levels(seeds[6], (VOCAB, D), ((0, 32),), -0.2, 0.2)), 6.679405834854324e-13, 1.0687049335766918e-11),
        "position_table": bell_draw(seeds[7], (NPOS, D), 0.05, 0.75, ((0, 32),), jnp.float32),
        "position_first": bell_draw(seeds[8], (NPOS, D), (0.01 / PARAMS ** 0.5), 1.52587890625e-05, ((0, 32),), jnp.float32),
        "position_second": jnp.clip(jnp.exp(math.log(1.0687049335766918e-11) - 2.7725887 * jax.random.uniform(seeds[9], (NPOS, D), jnp.float32) ** levels(seeds[9], (NPOS, D), ((0, 32),), -0.2, 0.2)), 6.679405834854324e-13, 1.0687049335766918e-11),
        "shared_wide": bell_draw(seeds[10], (D, 4 * D + FF), D ** -0.5, 0.21875, ((0, 32),), jnp.float32),
        "shared_wide_first": bell_draw(seeds[11], (D, 4 * D + FF), (0.01 / PARAMS ** 0.5), 1.52587890625e-05, ((0, 32),), jnp.float32),
        "shared_wide_second": jnp.clip(jnp.exp(math.log(1.0687049335766918e-11) - 2.7725887 * jax.random.uniform(seeds[12], (D, 4 * D + FF), jnp.float32) ** levels(seeds[12], (D, 4 * D + FF), ((0, 32),), -0.2, 0.2)), 6.679405834854324e-13, 1.0687049335766918e-11),
        "shared_down": bell_draw(seeds[13], (FF, D), FF ** -0.5, 0.109375, ((0, 32),), jnp.float32),
        "shared_down_first": bell_draw(seeds[14], (FF, D), (0.01 / PARAMS ** 0.5), 1.52587890625e-05, ((0, 32),), jnp.float32),
        "shared_down_second": jnp.clip(jnp.exp(math.log(1.0687049335766918e-11) - 2.7725887 * jax.random.uniform(seeds[15], (FF, D), jnp.float32) ** levels(seeds[15], (FF, D), ((0, 32),), -0.2, 0.2)), 6.679405834854324e-13, 1.0687049335766918e-11),
        "shared_vectors": draw_shared_vectors(jax.random.fold_in(seeds[28], 71), 0),
        "shared_vectors_first": bell_draw(seeds[17], (10 * D + FF,), (0.04 / PARAMS ** 0.5), 6.103515625e-05, ((0, 32),), jnp.float32),
        "shared_vectors_second": jnp.clip(jnp.exp(math.log(1.709927893722707e-10) - 2.7725887 * jax.random.uniform(seeds[18], (10 * D + FF,), jnp.float32) ** levels(seeds[18], (10 * D + FF,), ((0, 32),), -0.2, 0.2)), 1.0687049335766918e-11, 1.709927893722707e-10),
        "private_wide": bell_draw(seeds[19], (CLIENTS, D, 4 * D + FF), D ** -0.5, 0.21875, ((0, 4), (1, 8)), jnp.float32),
        "private_wide_first": bell_draw(seeds[20], (CLIENTS, D, 4 * D + FF), (0.01 / PARAMS ** 0.5), 1.52587890625e-05, ((0, 4), (1, 8)), jnp.float32),
        "private_wide_second": jnp.clip(jnp.exp(math.log(1.0687049335766918e-11) - 2.7725887 * jax.random.uniform(seeds[21], (CLIENTS, D, 4 * D + FF), jnp.float32) ** levels(seeds[21], (CLIENTS, D, 4 * D + FF), ((0, 4), (1, 8)), -0.2, 0.2)), 6.679405834854324e-13, 1.0687049335766918e-11),
        "private_down": bell_draw(seeds[22], (CLIENTS, FF, D), FF ** -0.5, 0.109375, ((0, 4), (1, 8)), jnp.float32),
        "private_down_first": bell_draw(seeds[23], (CLIENTS, FF, D), (0.01 / PARAMS ** 0.5), 1.52587890625e-05, ((0, 4), (1, 8)), jnp.float32),
        "private_down_second": jnp.clip(jnp.exp(math.log(1.0687049335766918e-11) - 2.7725887 * jax.random.uniform(seeds[24], (CLIENTS, FF, D), jnp.float32) ** levels(seeds[24], (CLIENTS, FF, D), ((0, 4), (1, 8)), -0.2, 0.2)), 6.679405834854324e-13, 1.0687049335766918e-11),
        "private_vectors": draw_private_vectors(jax.random.fold_in(seeds[28], 71), 0),
        "private_vectors_first": bell_draw(seeds[26], (CLIENTS, 8 * D + FF), (0.04 / PARAMS ** 0.5), 6.103515625e-05, ((0, 4), (1, 8)), jnp.float32),
        "private_vectors_second": jnp.clip(jnp.exp(math.log(1.709927893722707e-10) - 2.7725887 * jax.random.uniform(seeds[27], (CLIENTS, 8 * D + FF), jnp.float32) ** levels(seeds[27], (CLIENTS, 8 * D + FF), ((0, 4), (1, 8)), -0.2, 0.2)), 1.0687049335766918e-11, 1.709927893722707e-10),
    }


@jax.custom_vjp
def low(v):
    return lax.optimization_barrier(v.astype(jnp.bfloat16)).astype(jnp.float32)

@jax.custom_vjp
def low_back(v):
    return v

def low_keep(v):
    return (low(v), None)

def low_pass(kept, grad):
    return (grad,)

def back_keep(v):
    return (v, None)

def back_low(kept, grad):
    return (low(grad),)
low.defvjp(low_keep, low_pass)
low_back.defvjp(back_keep, back_low)
SCALE = 0.125
CLIP_NORM = 0.01
RATE_MATRIX = 0.03
RATE_VECTOR = 0.5
DECAY = 0.01
EPSILON = 1e-08

def product(former, latter):
    return jnp.dot(former, latter, precision=lax.Precision.HIGHEST, preferred_element_type=jnp.float32)

def layer_norm(values, scales, shifts):
    centre = values - lax.optimization_barrier(jnp.mean(values, -1, keepdims=True))
    spread = lax.optimization_barrier(jnp.mean(centre * centre, -1, keepdims=True))
    return centre * lax.rsqrt(spread + 1e-05) * scales + shifts

def split_vectors(vectors, breadth, hidden):
    starts = [0, breadth, 2 * breadth, 3 * breadth, 4 * breadth, 5 * breadth, 6 * breadth, 7 * breadth, 7 * breadth + hidden, 8 * breadth + hidden]
    return [vectors[starts[position]:starts[position + 1]] for position in range(9)]

def block(inputs, wide, down, vectors, live_len):
    breadth = inputs.shape[1]
    seq_len = inputs.shape[0]
    parts = split_vectors(vectors, breadth, down.shape[0])
    normed = low(layer_norm(inputs, parts[0], parts[1]))
    shift_qkv = jnp.concatenate([parts[2], jnp.zeros_like(parts[2]), parts[3]])
    joined = low(low_back(product(normed, wide[:, :3 * breadth]) + shift_qkv))
    triple = joined.reshape(seq_len, 3, breadth // HD, HD)
    scores = jnp.einsum('qhd,khd->hqk', triple[:, 0], triple[:, 1], precision=lax.Precision.HIGHEST) * SCALE
    rows_at = lax.broadcasted_iota(jnp.int32, (seq_len, seq_len), 0)
    cols_at = lax.broadcasted_iota(jnp.int32, (seq_len, seq_len), 1)
    allowed = (cols_at <= rows_at) & (cols_at < live_len)
    scores = low_back(jnp.where(allowed[None], scores, -1e+30))
    probs = jax.nn.softmax(scores, axis=-1)
    mixed_out = jnp.einsum('hqk,khd->qhd', low(probs), triple[:, 2], precision=lax.Precision.HIGHEST)
    mixed_out = low(low_back(mixed_out.reshape(seq_len, breadth)))
    middle = inputs + low_back(product(mixed_out, wide[:, 3 * breadth:4 * breadth]) + parts[4])
    normed_two = low(layer_norm(middle, parts[5], parts[6]))
    pre_act = low_back(product(normed_two, wide[:, 4 * breadth:]) + parts[7])
    activ = low(jax.nn.gelu(pre_act, approximate=True))
    return middle + low_back(product(activ, down) + parts[8])

def adamw(weight, first, second, gradient, rate, decay):
    first_new = 0.5 * first + 0.5 * gradient
    second_new = 0.5 * second + 0.5 * gradient * gradient
    first_hat = first_new / (1.0 - 0.5 ** STEP)
    second_hat = second_new / (1.0 - 0.5 ** STEP)
    weight_new = weight - rate * (first_hat / (jnp.sqrt(second_hat) + EPSILON) + decay * weight)
    return (weight_new, first_new, second_new)

def reference(token_ids, lengths, picked, joining, embedding, embedding_first, embedding_second, position_table, position_first, position_second, shared_wide, shared_wide_first, shared_wide_second, shared_down, shared_down_first, shared_down_second, shared_vectors, shared_vectors_first, shared_vectors_second, private_wide, private_wide_first, private_wide_second, private_down, private_down_first, private_down_second, private_vectors, private_vectors_first, private_vectors_second):
    live = picked < lengths[:, :, None] - 1
    counts = lax.optimization_barrier(jnp.sum(live.astype(jnp.float32), axis=(1, 2)))
    share = joining.astype(jnp.float32) / (jnp.sum(joining).astype(jnp.float32) * counts)
    seq_share = jnp.repeat(share, SEQS)
    seq_client = jnp.repeat(jnp.arange(CLIENTS, dtype=jnp.int32), SEQS)
    flat_ids = token_ids.reshape(CLIENTS * SEQS, LEN)
    flat_lengths = lengths.reshape(CLIENTS * SEQS)
    flat_picks = picked.reshape(CLIENTS * SEQS, PICK)
    params = (embedding, position_table, shared_wide, shared_down, shared_vectors, private_wide, private_down, private_vectors)

    def total_loss(weights):
        table_b, posit_b, wide_s, down_s, vect_s, wide_p, down_p, vect_p = [low(member) for member in weights]
        final_scale = vect_s[8 * D + FF:9 * D + FF]
        final_shift = vect_s[9 * D + FF:10 * D + FF]

        def one_sequence(carry, item):
            id_row, live_len, pick_row, seq_weight, client = item
            hidden_state = table_b[id_row] + posit_b[:LEN]
            hidden_state = block(hidden_state, wide_p[client], down_p[client], vect_p[client], live_len)
            hidden_state = block(hidden_state, wide_s, down_s, vect_s, live_len)
            final_b = low(layer_norm(hidden_state[pick_row], final_scale, final_shift))
            logits = low_back(product(final_b, table_b.T))
            log_total = jax.nn.logsumexp(logits, axis=-1)
            target = jnp.take_along_axis(logits, id_row[pick_row + 1][:, None], 1)[:, 0]
            raw_sum = jnp.sum(jnp.where(pick_row < live_len - 1, log_total - target, 0.0))
            return (carry + seq_weight * raw_sum, raw_sum)
        total, raws = lax.scan(jax.checkpoint(one_sequence), jnp.zeros((), jnp.float32), (flat_ids, flat_lengths, flat_picks, seq_share, seq_client))
        return (total, raws)
    total, backward, raws = jax.vjp(total_loss, params, has_aux=True)
    grads = backward(jnp.ones((), jnp.float32))[0]
    squares = jnp.zeros((), jnp.float32)
    for gradient in grads:
        squares = squares + jnp.sum(gradient * gradient)
    grad_norm = jnp.sqrt(squares)
    factor = jnp.minimum(1.0, CLIP_NORM / grad_norm)
    g_table, g_posit, g_wide_s, g_down_s, g_vect_s, g_wide_p, g_down_p, g_vect_p = [member * factor for member in grads]
    emb_new, emb_first, emb_second = adamw(embedding, embedding_first, embedding_second, g_table, RATE_MATRIX, DECAY)
    pos_new, pos_first, pos_second = adamw(position_table, position_first, position_second, g_posit, RATE_MATRIX, DECAY)
    sw_new, sw_first, sw_second = adamw(shared_wide, shared_wide_first, shared_wide_second, g_wide_s, RATE_MATRIX, DECAY)
    sd_new, sd_first, sd_second = adamw(shared_down, shared_down_first, shared_down_second, g_down_s, RATE_MATRIX, DECAY)
    sv_new, sv_first, sv_second = adamw(shared_vectors, shared_vectors_first, shared_vectors_second, g_vect_s, RATE_VECTOR, 0.0)
    pw_new, pw_first, pw_second = adamw(private_wide, private_wide_first, private_wide_second, g_wide_p, RATE_MATRIX, DECAY)
    pd_new, pd_first, pd_second = adamw(private_down, private_down_first, private_down_second, g_down_p, RATE_MATRIX, DECAY)
    pv_new, pv_first, pv_second = adamw(private_vectors, private_vectors_first, private_vectors_second, g_vect_p, RATE_VECTOR, 0.0)
    client_sums = lax.optimization_barrier(jnp.sum(raws.reshape(CLIENTS, SEQS), axis=1))
    return (emb_new, emb_first, emb_second, pos_new, pos_first, pos_second, sw_new, sw_first, sw_second, sd_new, sd_first, sd_second, sv_new, sv_first, sv_second, pw_new, pw_first, pw_second, pd_new, pd_first, pd_second, pv_new, pv_first, pv_second, client_sums, counts, grad_norm)
```

```python
import jax
import jax.numpy as jnp
from jax import lax
from jax.sharding import Mesh
from jax.sharding import PartitionSpec as P

HD = 64
D = 768
FF = 3072
NPOS = 1024
STEP = 5


SCALE = 0.125
CLIP_NORM = 0.01
RATE_MATRIX = 0.03
RATE_VECTOR = 0.5
DECAY = 0.01
EPSILON = 1e-08
BF = jnp.bfloat16
F32 = jnp.float32


def dot_plain(former, latter):
    return jnp.dot(former, latter, preferred_element_type=jnp.float32)


def dot_inner(former, latter):
    return lax.dot_general(
        former, latter, (((0,), (0,)), ((), ())), preferred_element_type=jnp.float32
    )


def dot_outer(former, latter):
    return lax.dot_general(
        former, latter, (((1,), (1,)), ((), ())), preferred_element_type=jnp.float32
    )


def layer_norm(values, scales, shifts):
    centre = values - jnp.mean(values, -1, keepdims=True)
    spread = jnp.mean(centre * centre, -1, keepdims=True)
    return centre * lax.rsqrt(spread + 1e-05) * scales + shifts


def gelu_tanh(values):
    return jax.nn.gelu(values, approximate=True)


def split_vectors(vectors, breadth, hidden):
    starts = [
        0,
        breadth,
        2 * breadth,
        3 * breadth,
        4 * breadth,
        5 * breadth,
        6 * breadth,
        7 * breadth,
        7 * breadth + hidden,
        8 * breadth + hidden,
    ]
    return [vectors[starts[position] : starts[position + 1]] for position in range(9)]


def causal_mask(seq_len, live_len):
    rows_at = lax.broadcasted_iota(jnp.int32, (seq_len, seq_len), 0)
    cols_at = lax.broadcasted_iota(jnp.int32, (seq_len, seq_len), 1)
    return (cols_at <= rows_at) & (cols_at < live_len)


def masked_scores(block_qkv, seq_len, live_len):
    scores = (
        jnp.einsum(
            "qhd,khd->hqk", block_qkv[:, 0], block_qkv[:, 1], preferred_element_type=jnp.float32
        )
        * SCALE
    )
    return jnp.where(causal_mask(seq_len, live_len)[None], scores, -1e30)


def attend(joined, live_len):
    breadth = joined.shape[1] // 3
    seq_len = joined.shape[0]
    block_qkv = joined.reshape(seq_len, 3, breadth // HD, HD)
    scores = masked_scores(block_qkv, seq_len, live_len)
    highest = jnp.max(scores, -1, keepdims=True)
    exponent = jnp.exp(scores - highest)
    totals = jnp.sum(exponent, -1, keepdims=True)
    probs_b = (exponent / totals).astype(jnp.bfloat16)
    mixed_out = jnp.einsum(
        "hqk,khd->qhd", probs_b, block_qkv[:, 2], preferred_element_type=jnp.float32
    )
    return (
        mixed_out.astype(jnp.bfloat16).reshape(seq_len, breadth),
        (highest + jnp.log(totals))[..., 0],
    )


def attend_back(joined, log_total, grad_mixed, live_len):
    breadth = joined.shape[1] // 3
    seq_len = joined.shape[0]
    head_count = breadth // HD
    block_qkv = joined.reshape(seq_len, 3, head_count, HD)
    grad_out = grad_mixed.reshape(seq_len, head_count, HD)
    scores = masked_scores(block_qkv, seq_len, live_len)
    probs = jnp.exp(scores - log_total[..., None])
    probs_b = probs.astype(jnp.bfloat16)
    grad_values = jnp.einsum("hqk,qhd->khd", probs_b, grad_out, preferred_element_type=jnp.float32)
    grad_probs = jnp.einsum(
        "qhd,khd->hqk", grad_out, block_qkv[:, 2], preferred_element_type=jnp.float32
    )
    inner = jnp.sum(grad_probs * probs, -1, keepdims=True)
    grad_scores = (probs * (grad_probs - inner)).astype(jnp.bfloat16)
    grad_queries = (
        jnp.einsum("hqk,khd->qhd", grad_scores, block_qkv[:, 1], preferred_element_type=jnp.float32)
        * SCALE
    )
    grad_keys = (
        jnp.einsum("hqk,qhd->khd", grad_scores, block_qkv[:, 0], preferred_element_type=jnp.float32)
        * SCALE
    )
    stacked = jnp.stack([grad_queries, grad_keys, grad_values], 1).astype(jnp.bfloat16)
    return stacked.reshape(seq_len, 3 * breadth)


def layer_forward(inputs, weights, vectors, live_len):
    qkvo, fore, down = weights
    breadth = inputs.shape[1]
    parts = split_vectors(vectors, breadth, down.shape[0])
    normed = layer_norm(inputs, parts[0], parts[1]).astype(jnp.bfloat16)
    shift_qkv = jnp.concatenate([parts[2], jnp.zeros_like(parts[2]), parts[3]])
    joined = (dot_plain(normed, qkvo[:, : 3 * breadth]) + shift_qkv).astype(jnp.bfloat16)
    mixed_out, log_totals = attend(joined, live_len)
    middle = inputs + (dot_plain(mixed_out, qkvo[:, 3 * breadth :]) + parts[4])
    normed_two = layer_norm(middle, parts[5], parts[6]).astype(jnp.bfloat16)
    pre_act = dot_plain(normed_two, fore) + parts[7]
    activ = gelu_tanh(pre_act).astype(jnp.bfloat16)
    output = middle + (dot_plain(activ, down) + parts[8])
    return (
        output,
        (inputs, normed, joined, mixed_out, log_totals, middle, normed_two, pre_act, activ),
    )


def layer_backward(grad_out, saved, weights, vectors, live_len):
    inputs, normed, joined, mixed_out, log_totals, middle, normed_two, pre_act, activ = saved
    qkvo, fore, down = weights
    breadth = inputs.shape[1]
    parts = split_vectors(vectors, breadth, down.shape[0])
    grad_y = grad_out.astype(jnp.bfloat16)
    grad_down = dot_inner(activ, grad_y).astype(BF)
    grad_act = dot_outer(grad_y, down)
    grad_pre = jax.vjp(gelu_tanh, pre_act)[1](grad_act)[0].astype(jnp.bfloat16)
    grad_fore = dot_inner(normed_two, grad_pre).astype(BF)
    grad_norm_two = dot_outer(grad_pre, fore)
    grad_mid_norm, grad_scale_two, grad_shift_two = jax.vjp(layer_norm, middle, parts[5], parts[6])[
        1
    ](grad_norm_two)
    grad_mid = grad_out + grad_mid_norm
    grad_branch = grad_mid.astype(jnp.bfloat16)
    grad_proj = dot_inner(mixed_out, grad_branch).astype(BF)
    grad_mixed = dot_outer(grad_branch, qkvo[:, 3 * breadth :]).astype(jnp.bfloat16)
    grad_joined = attend_back(joined, log_totals, grad_mixed, live_len)
    grad_qkv = dot_inner(normed, grad_joined).astype(BF)
    grad_normed = dot_outer(grad_joined, qkvo[:, : 3 * breadth])
    grad_in_norm, grad_scale_one, grad_shift_one = jax.vjp(layer_norm, inputs, parts[0], parts[1])[
        1
    ](grad_normed)
    joined_sums = jnp.sum(grad_joined.astype(jnp.float32), 0)
    grad_vectors = jnp.concatenate(
        [
            grad_scale_one,
            grad_shift_one,
            joined_sums[:breadth],
            joined_sums[2 * breadth :],
            jnp.sum(grad_branch.astype(jnp.float32), 0),
            grad_scale_two,
            grad_shift_two,
            jnp.sum(grad_pre.astype(jnp.float32), 0),
            jnp.sum(grad_y.astype(jnp.float32), 0),
        ]
    )
    grad_qkvo = jnp.concatenate([grad_qkv, grad_proj], 1)
    return (grad_mid + grad_in_norm, (grad_qkvo, grad_fore, grad_down), grad_vectors)


def adamw(weight, first, second, gradient, rate, decay):
    first_new = 0.5 * first + 0.5 * gradient
    second_new = 0.5 * second + 0.5 * gradient * gradient
    first_hat = first_new / (1.0 - 0.5**STEP)
    second_hat = second_new / (1.0 - 0.5**STEP)
    weight_new = weight - rate * (first_hat / (jnp.sqrt(second_hat) + EPSILON) + decay * weight)
    return (weight_new, first_new, second_new)


FLIP = [(0, 1), (1, 0)]


def across(x, name):
    return lax.ppermute(x, name, FLIP)


def gather_bit(x, name, dim):
    other = across(x, name)
    low_side = lax.axis_index(name) == 0
    return jnp.where(
        low_side, jnp.concatenate([x, other], dim), jnp.concatenate([other, x], dim)
    )


def gather_bits(x, names, order):
    x = x.reshape((1,) * len(names) + x.shape)
    for name in order:
        x = gather_bit(x, name, names.index(name))
    x = x.reshape((-1,) + x.shape[len(names) :])
    return x.reshape((x.shape[0] * x.shape[1],) + x.shape[2:])


def reduce_bit(x, name, dim, last=BF):
    side = lax.axis_index(name)
    keep = lax.dynamic_index_in_dim(x, side, dim, True)
    other = across(lax.dynamic_index_in_dim(x, 1 - side, dim, True), name)
    return (keep.astype(F32) + other.astype(F32)).astype(last)


def reduce_bits(x, names, order):
    shape = x.shape
    x = x.reshape((2,) * len(names) + (shape[0] // 2 ** len(names),) + shape[1:])
    for name in order:
        x = reduce_bit(x, name, names.index(name), F32 if name == order[-1] else BF)
    return x.reshape((-1,) + shape[1:])


def sum_bits(x, names):
    for name in names:
        x = x + across(x, name)
    return x


def per_device(
    shard_names,
    token_ids,
    lengths,
    picked,
    joining,
    embedding,
    embedding_first,
    embedding_second,
    position_table,
    position_first,
    position_second,
    shared_wide,
    shared_wide_first,
    shared_wide_second,
    shared_down,
    shared_down_first,
    shared_down_second,
    shared_vectors,
    shared_vectors_first,
    shared_vectors_second,
    private_wide,
    private_wide_first,
    private_wide_second,
    private_down,
    private_down_first,
    private_down_second,
    private_vectors,
    private_vectors_first,
    private_vectors_second,
):
    half, rest = shard_names[0], shard_names[1:]
    every = ("pair", "core") + shard_names
    crew = ("core",) + rest
    shards = 2 ** len(shard_names)
    clients = 4
    count = clients * shards
    at_pair, at_core, at_half = (lax.axis_index(n) for n in ("pair", "core", half))
    device_at = lax.axis_index(every)
    shard_at = lax.axis_index(shard_names)
    swap_pairs = []
    block = shards // 2
    for pair in range(clients // 2):
        for spot in range(block):
            former = ((pair * 2 + 0) * 2 + 1) * block + spot
            latter = ((pair * 2 + 1) * 2 + 0) * block + spot
            swap_pairs += [(former, latter), (latter, former)]

    def swap(x):
        return jnp.where(at_core == at_half, x, lax.ppermute(x, every, swap_pairs))

    seq_len = token_ids.shape[2]
    picks = picked.shape[2]
    slice_rows = embedding.shape[0]

    wide_b = private_wide[0].astype(BF)
    down_b = private_down[0].astype(BF)
    there, back = crew[1:] + ("core",), crew[:0:-1] + ("core",)
    cut = 4 * D
    weights_p = (
        gather_bits(swap(wide_b[:, :cut]), crew, there),
        gather_bits(swap(wide_b[:, cut:]), crew, back),
        gather_bits(swap(down_b), crew, there),
    )
    shared_b = shared_wide.astype(BF)
    spread = shard_names + ("pair", "core")
    weights_s = (
        gather_bits(shared_b[:, :cut], every, spread),
        gather_bits(shared_b[:, cut:], every, spread),
        gather_bits(shared_down.astype(BF), every, spread),
    )
    posit_b = gather_bits(position_table.astype(BF), every, spread)[:seq_len]
    table_own = embedding.astype(BF)
    table_four = gather_bits(table_own, ("pair", "core"), ("pair", "core"))

    ids = token_ids[0, 0]
    same = ids[:, None] == ids[None, :]
    at_row = lax.broadcasted_iota(jnp.int32, (seq_len, seq_len), 0)
    at_col = lax.broadcasted_iota(jnp.int32, (seq_len, seq_len), 1)
    first_at = jnp.min(jnp.where(same, at_col, seq_len), 1)
    is_first = first_at == jnp.arange(seq_len, dtype=jnp.int32)
    owners = ids // slice_rows
    slot = jnp.sum(
        (
            (owners[:, None] == owners[None, :]) & is_first[None, :] & (at_col < first_at[:, None])
        ).astype(jnp.int32),
        1,
    )

    vect_own = [shared_vectors, private_vectors[0]]
    pieces = [
        ids.astype(F32),
        slot.astype(F32),
        is_first.astype(F32),
        picked[0, 0].astype(F32),
        lengths[0].astype(F32),
    ] + [v.astype(BF).astype(F32) for v in vect_own]
    starts = [0]
    for piece in pieces:
        starts.append(starts[-1] + piece.shape[0])
    message = jnp.concatenate(pieces)
    message = jnp.pad(message, (0, -message.shape[0] % 1024)).reshape(1, -1, 128)
    board = lax.all_to_all(
        jnp.broadcast_to(message, (count,) + message.shape[1:]), every, 0, 0, tiled=True
    ).reshape(count, -1)

    def posted(place):
        return board[:, starts[place] : starts[place + 1]]

    def hosted(x):
        x = x.reshape((clients // 2, 2, 2, block) + x.shape[1:])
        return jnp.swapaxes(x, 1, 2).reshape((count,) + x.shape[4:])

    all_ids, all_slots, all_first, all_picks, all_lens = [
        hosted(posted(place).astype(jnp.int32)) for place in range(5)
    ]
    vect_s = posted(5).reshape(-1)
    vect_p = lax.dynamic_index_in_dim(
        posted(6).reshape(clients, -1), 2 * at_pair + at_half, 0, False
    )

    all_live = all_picks < all_lens - 1
    live_counts = jnp.sum(all_live.astype(F32), 1).reshape(clients // 2, 2, 2, block)
    counts_all = jnp.sum(live_counts, (1, 3)).reshape(-1)
    joining_f = joining.astype(F32)
    share_all = joining_f / (jnp.sum(joining_f) * counts_all)

    my_ids = lax.dynamic_index_in_dim(all_ids, device_at, 0, False)
    my_slots = lax.dynamic_index_in_dim(all_slots, device_at, 0, False)
    my_picks = lax.dynamic_index_in_dim(all_picks, device_at, 0, False)
    my_len = lax.dynamic_index_in_dim(all_lens, device_at, 0, False)[0]
    my_owners = my_ids // slice_rows

    room = max(16, 1024 // count)
    rounds = jnp.max(all_slots) // room + 1
    in_slice = all_ids - device_at * slice_rows
    wanted = (all_first > 0) & (in_slice >= 0) & (in_slice < slice_rows)

    def asked(turn):
        spots = turn * room + jnp.arange(room, dtype=jnp.int32)
        hits = wanted[:, None, :] & (all_slots[:, None, :] == spots[None, :, None])
        return jnp.sum(jnp.where(hits, in_slice[:, None, :], 0), 2).reshape(-1)

    def fetch(turn, rows):
        sent = jnp.take(table_own, asked(turn), axis=0, mode="clip")
        got = lax.all_to_all(sent, every, 0, 0, tiled=True)
        spot = my_slots - turn * room
        here = (spot >= 0) & (spot < room)
        found = jnp.take(got, jnp.where(here, my_owners * room + spot, 0), axis=0, mode="clip")
        return jnp.where(here[:, None], found, rows)

    rows = fetch(0, jnp.zeros((seq_len, D), BF))
    rows = lax.fori_loop(1, rounds, fetch, rows)
    inputs = rows.astype(F32) + posit_b.astype(F32)

    first_out, first_saved = layer_forward(inputs, weights_p, vect_p, my_len)
    second_out, second_saved = layer_forward(first_out, weights_s, vect_s[: 8 * D + FF], my_len)

    final_scale = vect_s[8 * D + FF : 9 * D + FF]
    final_shift = vect_s[9 * D + FF : 10 * D + FF]
    final_in = jnp.take(second_out, my_picks, axis=0, mode="clip")
    final_b = layer_norm(final_in, final_scale, final_shift).astype(BF)
    target_rows = jnp.take(rows, my_picks + 1, axis=0, mode="clip").astype(F32)

    scored = gather_bits(final_b, shard_names, shard_names)

    def group(x):
        x = x.reshape((clients, shards) + x.shape[1:])
        return lax.dynamic_index_in_dim(x, 2 * at_pair + at_core, 0, False)

    group_ids, group_picks, group_live = group(all_ids), group(all_picks), group(all_live)
    seq_at = lax.broadcasted_iota(jnp.int32, (shards, picks, seq_len), 2)
    targets = jnp.sum(
        jnp.where(seq_at == group_picks[:, :, None] + 1, group_ids[:, None, :], 0), 2
    ).reshape(-1)
    host_clients = 2 * at_pair + jnp.arange(shards, dtype=jnp.int32) // block
    weight = jnp.where(group_live, jnp.take(share_all, host_clients)[:, None], 0.0).reshape(-1)
    target_owner = targets // slice_rows
    local_target = jnp.where(
        target_owner % shards == shard_at,
        target_owner // shards * slice_rows + targets % slice_rows,
        -1,
    )
    logits = dot_outer(scored, table_four)
    hit = lax.broadcasted_iota(jnp.int32, logits.shape, 1) == local_target[:, None]
    part_max = jnp.max(logits, -1)
    exponent = jnp.exp(logits - part_max[:, None])
    part_sum = jnp.sum(exponent, -1)
    part_target = jnp.sum(jnp.where(hit, logits, 0.0), -1)
    pulled = dot_plain(exponent.astype(BF), table_four)
    top, total, target_logit = part_max, part_sum, part_target
    for name in shard_names:
        stats = across(jnp.stack([top, total, target_logit]), name)
        higher = jnp.maximum(top, stats[0])
        total = total * jnp.exp(top - higher) + stats[1] * jnp.exp(stats[0] - higher)
        top, target_logit = higher, target_logit + stats[2]
    log_all = top + jnp.log(total)
    pulled = (pulled * (weight * jnp.exp(part_max - log_all))[:, None]).astype(BF)
    pulled_own = reduce_bits(pulled, shard_names, shard_names[::-1])

    def own_rows(x):
        return lax.dynamic_slice_in_dim(x, shard_at * picks, picks, 0)

    own_weight = own_rows(weight)
    grad_final_b = pulled_own - own_weight[:, None] * target_rows
    own_live = lax.dynamic_index_in_dim(group_live, shard_at, 0, False)
    own_terms = jnp.sum(jnp.where(own_live, own_rows(log_all - target_logit), 0.0))
    grad_logits = (
        weight[:, None] * jnp.exp(logits - log_all[:, None])
        - jnp.where(hit, weight[:, None], 0.0)
    ).astype(BF)
    head_part = dot_inner(grad_logits, scored).astype(BF)
    head_own = reduce_bits(head_part, ("pair", "core"), ("core", "pair"))

    grad_final_in, grad_fscale, grad_fshift = jax.vjp(
        layer_norm, final_in, final_scale, final_shift
    )[1](grad_final_b)
    grad_second = jnp.zeros_like(second_out).at[my_picks].add(grad_final_in)
    grad_first, grads_s, grad_vect_s = layer_backward(
        grad_second, second_saved, weights_s, vect_s[: 8 * D + FF], my_len
    )
    gather_back = ("core", "pair") + shard_names[::-1]
    g_qkvo_s, g_fore_s, g_down_s = [reduce_bits(g, every, gather_back) for g in grads_s]
    grad_inputs, grads_p, grad_vect_p = layer_backward(
        grad_first, first_saved, weights_p, vect_p, my_len
    )
    g_qkvo_p, g_fore_p, g_down_p = [
        swap(reduce_bits(g, crew, order).astype(BF)).astype(F32)
        for g, order in zip(grads_p, (there[::-1], back[::-1], there[::-1]))
    ]

    vector_s = jnp.concatenate([grad_vect_s, grad_fscale, grad_fshift]).reshape(count, -1)
    to_client = jnp.arange(clients, dtype=jnp.int32) == 2 * at_pair + at_half
    vector_p = jnp.where(
        to_client[:, None, None], grad_vect_p.reshape(1, shards, -1), 0.0
    ).reshape(count, -1)
    width_s, width_p = vector_s.shape[1], vector_p.shape[1]
    packet = jnp.concatenate([vector_s, vector_p], 1)
    packet = jnp.pad(packet, ((0, 0), (0, -packet.shape[1] % 1024)))
    landed = lax.all_to_all(packet.reshape(count, -1, 128), every, 0, 0, tiled=True)
    landed = jnp.sum(landed.reshape(count, -1), 0)
    grad_vect_sh = landed[:width_s]
    grad_vect_ph = landed[width_s : width_s + width_p]

    posit_names = ("core",) + shard_names
    grad_posit = reduce_bits(grad_inputs.astype(BF), posit_names, posit_names)
    grad_posit = grad_posit + across(grad_posit.astype(BF), "pair").astype(F32)
    grad_posit = jnp.where(at_pair == 0, grad_posit, 0.0)

    grad_rows = grad_inputs.astype(BF)

    def give(turn, total_rows):
        spot = my_slots - turn * room
        here = (spot >= 0) & (spot < room)
        place = jnp.where(here, my_owners * room + spot, -1)
        chosen = lax.broadcasted_iota(jnp.int32, (count * room, seq_len), 0) == place[None, :]
        sent = dot_plain(chosen.astype(BF), grad_rows).astype(BF)
        got = lax.all_to_all(sent, every, 0, 0, tiled=True)
        landing = lax.broadcasted_iota(
            jnp.int32, (slice_rows, count * room), 0
        ) == asked(turn)[None, :]
        return total_rows + dot_plain(landing.astype(BF), got)

    grad_table = give(0, head_own)
    grad_table = lax.fori_loop(1, rounds, give, grad_table)

    all_grads = [
        grad_table,
        grad_posit,
        jnp.concatenate([g_qkvo_s, g_fore_s], 1),
        g_down_s,
        grad_vect_sh,
        jnp.concatenate([g_qkvo_p, g_fore_p], 1)[None],
        g_down_p[None],
        grad_vect_ph[None],
    ]
    squares = jnp.zeros((), jnp.float32)
    for gradient in all_grads:
        squares = squares + jnp.sum(gradient * gradient)
    client_at = jnp.arange(clients, dtype=jnp.int32)
    loss_vector = jnp.where(client_at == 2 * at_pair + at_half, own_terms, 0.0)
    figures = jnp.pad(jnp.concatenate([squares[None], loss_vector]), (0, 127 - clients))
    figures = sum_bits(figures, every)
    grad_norm = jnp.sqrt(figures[0])
    own_client = client_at == 2 * at_pair + at_core
    loss_sum = jnp.sum(jnp.where(own_client, figures[1 : 1 + clients], 0.0))
    count_sum = jnp.sum(jnp.where(own_client, counts_all, 0.0))
    factor = jnp.minimum(1.0, CLIP_NORM / grad_norm)
    g_table, g_posit, g_wide_s, g_down_s, g_vect_s, g_wide_p, g_down_p, g_vect_p = [
        member * factor for member in all_grads
    ]
    results = []
    for state, gradient, rate, decay in (
        ((embedding, embedding_first, embedding_second), g_table, RATE_MATRIX, DECAY),
        ((position_table, position_first, position_second), g_posit, RATE_MATRIX, DECAY),
        ((shared_wide, shared_wide_first, shared_wide_second), g_wide_s, RATE_MATRIX, DECAY),
        ((shared_down, shared_down_first, shared_down_second), g_down_s, RATE_MATRIX, DECAY),
        ((shared_vectors, shared_vectors_first, shared_vectors_second), g_vect_s, RATE_VECTOR, 0.0),
        ((private_wide, private_wide_first, private_wide_second), g_wide_p, RATE_MATRIX, DECAY),
        ((private_down, private_down_first, private_down_second), g_down_p, RATE_MATRIX, DECAY),
        (
            (private_vectors, private_vectors_first, private_vectors_second),
            g_vect_p,
            RATE_VECTOR,
            0.0,
        ),
    ):
        results += adamw(*state, gradient, rate, decay)
    return (*results, loss_sum.reshape(1), count_sum.reshape(1), grad_norm)


def solution(mesh):
    clients, shards = mesh.shape["client"], mesh.shape["shard"]
    depth = shards.bit_length() - 1
    if clients != 4 or shards != 2**depth:
        raise ValueError("mesh sizes")
    shard_names = tuple("s%d" % place for place in range(depth))
    fine = Mesh(
        mesh.devices.reshape((clients // 2, 2) + (2,) * depth), ("pair", "core") + shard_names
    )
    client, shard, both = ("pair", "core"), shard_names, ("pair", "core") + shard_names
    table, block, vector, lot = P(both, None), P(client, shard, None), P(both), P(client, shard)
    in_specs = (
        (block, lot, block, P())
        + (table,) * 12
        + (vector,) * 3
        + (block,) * 6
        + (lot,) * 3
    )
    out_specs = (
        (table,) * 12 + (vector,) * 3 + (block,) * 6 + (lot,) * 3 + (P(client), P(client), P())
    )

    def run(*arrays):
        return per_device(shard_names, *arrays)

    return jax.shard_map(
        run, mesh=fine, in_specs=in_specs, out_specs=out_specs, check_vma=False
    )
```

```python
import jax
import jax.numpy as jnp
from jax import lax
from jax.experimental import pallas as pl
from jax.experimental.pallas import tpu as pltpu
from jax.sharding import Mesh
from jax.sharding import PartitionSpec as P

HD = 64
D = 768
FF = 3072
NPOS = 1024
STEP = 5


SCALE = 0.125
CLIP_NORM = 0.01
RATE_MATRIX = 0.03
RATE_VECTOR = 0.5
DECAY = 0.01
EPSILON = 1e-08
BF = jnp.bfloat16
F32 = jnp.float32
NT = (((1,), (1,)), ((), ()))
TN = (((0,), (0,)), ((), ()))


def dot_plain(former, latter):
    return jnp.dot(former, latter, preferred_element_type=jnp.float32)


def dot_inner(former, latter):
    return lax.dot_general(
        former, latter, (((0,), (0,)), ((), ())), preferred_element_type=jnp.float32
    )


def dot_outer(former, latter):
    return lax.dot_general(
        former, latter, (((1,), (1,)), ((), ())), preferred_element_type=jnp.float32
    )


def layer_norm(values, scales, shifts):
    centre = values - jnp.mean(values, -1, keepdims=True)
    spread = jnp.mean(centre * centre, -1, keepdims=True)
    return centre * lax.rsqrt(spread + 1e-05) * scales + shifts


def gelu_tanh(values):
    return jax.nn.gelu(values, approximate=True)


def split_vectors(vectors, breadth, hidden):
    starts = [
        0,
        breadth,
        2 * breadth,
        3 * breadth,
        4 * breadth,
        5 * breadth,
        6 * breadth,
        7 * breadth,
        7 * breadth + hidden,
        8 * breadth + hidden,
    ]
    return [vectors[starts[position] : starts[position + 1]] for position in range(9)]


def product(former, latter, form):
    return lax.dot_general(former, latter, form, preferred_element_type=F32)


def write_mask(live_ref, mask_ref):
    keys = lax.broadcasted_iota(jnp.int32, mask_ref.shape, 0)
    queries = lax.broadcasted_iota(jnp.int32, mask_ref.shape, 1)
    allowed = (keys <= queries) & (keys < live_ref[0])
    mask_ref[...] = jnp.where(allowed, 0.0, -1e30)


def attend_kernel(live_ref, q_ref, k_ref, v_ref, out_ref, log_ref, mask_ref):
    @pl.when(pl.program_id(0) == 0)
    def _():
        write_mask(live_ref, mask_ref)

    tokens, width = q_ref.shape
    tile = tokens // 2
    for head in range(width // HD):
        cols = slice(head * HD, (head + 1) * HD)
        queries, keys, values = q_ref[:, cols] * SCALE, k_ref[:, cols], v_ref[:, cols]
        for part in range(2):
            begin, end = part * tile, (part + 1) * tile
            scores = product(keys[:end], queries[begin:end], NT) + mask_ref[:end, begin:end]
            highest = jnp.max(scores, 0, keepdims=True)
            exponent = jnp.exp(scores - highest)
            total = jnp.sum(exponent, 0, keepdims=True)
            probs = (exponent * (1.0 / total)).astype(BF)
            mixed = product(values[:end], probs, TN)
            out_ref[begin:end, cols] = mixed.T.astype(BF)
            log_ref[0, head : head + 1, begin:end] = highest + jnp.log(total)


def attend_back_kernel(live_ref, q_ref, k_ref, v_ref, grad_ref, log_ref, out_ref, mask_ref):
    @pl.when(pl.program_id(0) == 0)
    def _():
        write_mask(live_ref, mask_ref)

    tokens, width = q_ref.shape
    tile = tokens // 2
    breadth = out_ref.shape[1] // 3
    sides = [[], [], []]
    for head in range(width // HD):
        cols = slice(head * HD, (head + 1) * HD)
        queries, keys, values = q_ref[:, cols] * SCALE, k_ref[:, cols], v_ref[:, cols]
        grads = grad_ref[:, cols]
        grad_queries, grad_keys, grad_values = [], [], []
        for part in range(2):
            begin, end = part * tile, (part + 1) * tile
            scores = product(keys[:end], queries[begin:end], NT) + mask_ref[:end, begin:end]
            probs = jnp.exp(scores - log_ref[0, head : head + 1, begin:end])
            grad_out = grads[begin:end]
            grad_values.append(
                jnp.dot(probs.astype(BF), grad_out, preferred_element_type=F32)
            )
            grad_probs = product(values[:end], grad_out, NT)
            inner = jnp.sum(grad_probs * probs, 0, keepdims=True)
            grad_scores = (probs * (grad_probs - inner)).astype(BF)
            grad_keys.append(
                jnp.dot(grad_scores, queries[begin:end], preferred_element_type=F32)
            )
            grad_queries.append(product(keys[:end], grad_scores, TN).T * SCALE)
        for side, parts in ((1, grad_keys), (2, grad_values)):
            sides[side].append(
                jnp.concatenate([parts[0] + parts[1][:tile], parts[1][tile:]], 0)
            )
        sides[0].append(jnp.concatenate(grad_queries, 0))
    place = pl.program_id(0) * width
    for side in range(3):
        start = pl.multiple_of(side * breadth + place, width)
        out_ref[:, pl.ds(start, width)] = jnp.concatenate(sides[side], 1).astype(BF)


def attend(joined, live_len):
    tokens, breadth = joined.shape[0], joined.shape[1] // 3
    width = 2 * HD
    pairs = breadth // width
    parts = [
        pl.BlockSpec((tokens, width), lambda i, n, side=side: (0, side * pairs + i))
        for side in range(3)
    ]
    return pl.pallas_call(
        attend_kernel,
        grid_spec=pltpu.PrefetchScalarGridSpec(
            num_scalar_prefetch=1,
            grid=(pairs,),
            in_specs=parts,
            out_specs=[
                pl.BlockSpec((tokens, width), lambda i, n: (0, i)),
                pl.BlockSpec((1, 2, tokens), lambda i, n: (i, 0, 0)),
            ],
            scratch_shapes=[pltpu.VMEM((tokens, tokens), F32)],
        ),
        out_shape=[
            jax.ShapeDtypeStruct((tokens, breadth), BF),
            jax.ShapeDtypeStruct((pairs, 2, tokens), F32),
        ],
        compiler_params=pltpu.CompilerParams(vmem_limit_bytes=32 << 20),
        cost_estimate=pl.CostEstimate(
            flops=4 * tokens * tokens * breadth,
            bytes_accessed=8 * tokens * breadth,
            transcendentals=tokens * tokens * breadth // HD,
        ),
    )(live_len.reshape(1), joined, joined, joined)


def attend_back(joined, log_total, grad_mixed, live_len):
    tokens, breadth = grad_mixed.shape
    width = 2 * HD
    pairs = breadth // width
    parts = [
        pl.BlockSpec((tokens, width), lambda i, n, side=side: (0, side * pairs + i))
        for side in range(3)
    ]
    return pl.pallas_call(
        attend_back_kernel,
        grid_spec=pltpu.PrefetchScalarGridSpec(
            num_scalar_prefetch=1,
            grid=(pairs,),
            in_specs=parts
            + [
                pl.BlockSpec((tokens, width), lambda i, n: (0, i)),
                pl.BlockSpec((1, 2, tokens), lambda i, n: (i, 0, 0)),
            ],
            out_specs=pl.BlockSpec((tokens, 3 * breadth), lambda i, n: (0, 0)),
            scratch_shapes=[pltpu.VMEM((tokens, tokens), F32)],
        ),
        out_shape=jax.ShapeDtypeStruct((tokens, 3 * breadth), BF),
        compiler_params=pltpu.CompilerParams(vmem_limit_bytes=32 << 20),
        cost_estimate=pl.CostEstimate(
            flops=10 * tokens * tokens * breadth,
            bytes_accessed=14 * tokens * breadth,
            transcendentals=tokens * tokens * breadth // HD,
        ),
    )(live_len.reshape(1), joined, joined, joined, grad_mixed, log_total)


def fence(*arrays):
    return lax.optimization_barrier(arrays)


class Tree:
    def tied(self):
        return [self.held] if self.other is None else [self.held, self.other]

    def retie(self, arrays):
        self.held = arrays[0]
        if self.other is not None:
            self.other = arrays[1]

    def step(self):
        if self.other is None:
            self.send()
        else:
            self.advance()

    def result(self):
        while self.open:
            self.step()
        return self.final()


class Gather(Tree):
    def __init__(self, block, names, order, waits=(), lazy=False):
        self.names, self.order, self.rows, self.waits = names, list(order), block.shape, list(waits)
        self.held = block.reshape((1,) * len(names) + block.shape)
        self.other = None
        if not lazy:
            self.send()

    def send(self):
        self.other = across(self.held, self.order[0])

    def advance(self):
        name = self.order.pop(0)
        dim, low_side = self.names.index(name), lax.axis_index(name) == 0
        self.held = jnp.where(
            low_side,
            jnp.concatenate([self.held, self.other], dim),
            jnp.concatenate([self.other, self.held], dim),
        )
        self.other = None
        if self.order:
            self.send()

    @property
    def open(self):
        return bool(self.order)

    def final(self):
        return self.held.reshape((-1,) + self.rows[1:])


class Reduce(Tree):
    def __init__(self, blocks, names, order, after=None, waits=(), lazy=False):
        self.names, self.order, self.after, self.waits = names, list(order), after, list(waits)
        self.tail = blocks.shape[1:]
        self.held = blocks.reshape((2,) * len(names) + (-1,) + self.tail)
        self.other = None
        if not lazy:
            self.send()

    def send(self):
        if self.order:
            name = self.order[0]
            dim, side = self.names.index(name), lax.axis_index(name)
            self.other = across(lax.dynamic_index_in_dim(self.held, 1 - side, dim, True), name)
            self.held = lax.dynamic_index_in_dim(self.held, side, dim, True)
        else:
            self.held = self.held.astype(BF)
            self.other = self.after[0](self.held)

    def advance(self):
        if self.order:
            self.order.pop(0)
            total = self.held.astype(F32) + self.other.astype(F32)
            self.held = total.astype(BF) if self.order else total
        else:
            self.held = self.after[1](self.held, self.other)
            self.after = None
        self.other = None
        if self.open:
            self.send()

    @property
    def open(self):
        return bool(self.order) or self.after is not None

    def final(self):
        return self.held.astype(F32).reshape((-1,) + self.tail)


class Exchange(Tree):
    def __init__(self, packet, names, waits):
        self.held, self.names, self.waits = packet, names, list(waits)
        self.other, self.open = None, True

    def send(self):
        self.other = lax.all_to_all(self.held, self.names, 0, 0, tiled=True)

    def advance(self):
        self.open = False

    def final(self):
        return self.other


def meet(carry, trees):
    due = []
    for tree in trees:
        if tree.open:
            if tree.waits and tree.waits[0] > 0:
                tree.waits[0] -= 1
            else:
                tree.waits = tree.waits[1:]
                due.append(tree)
    flat, spans = list(carry), []
    for tree in due:
        start = len(flat)
        flat += tree.tied()
        spans.append((start, len(flat)))
    flat = fence(*flat)
    for tree, (start, stop) in zip(due, spans):
        tree.retie(flat[start:stop])
        tree.step()
    return flat[: len(carry)]


def core_half(active, lead, side):
    width = active.shape[1] // (2 * lead)
    if width % 128:
        pieces = [
            active[:, (2 * part + core) * width : (2 * part + core + 1) * width]
            for core in range(2)
            for part in range(lead)
        ]
        active, lead, width = jnp.concatenate(pieces, 1), 1, width * lead
    pieces = [
        lax.dynamic_slice_in_dim(active, (2 * part + side) * width, width, 1)
        for part in range(lead)
    ]
    return pieces[0] if lead == 1 else jnp.concatenate(pieces, 1)


def core_reduce(active, grad, lead):
    side = lax.axis_index("core")
    send = dot_inner(core_half(active, lead, 1 - side), grad).astype(BF)
    other = across(send, "core")
    return (dot_inner(core_half(active, lead, side), grad) + other.astype(F32)).astype(BF)


def settled(weight):
    return weight.result() if isinstance(weight, Tree) else weight


def layer_forward(inputs, weights, vectors, live_len, meets):
    breadth = inputs.shape[1]
    parts = split_vectors(vectors, breadth, vectors.shape[0] - 8 * breadth)
    normed = layer_norm(inputs, parts[0], parts[1]).astype(jnp.bfloat16)
    shift_qkv = jnp.concatenate([parts[2], jnp.zeros_like(parts[2]), parts[3]])
    qkvo = settled(weights[0])
    joined = (dot_plain(normed, qkvo[:, : 3 * breadth]) + shift_qkv).astype(jnp.bfloat16)
    mixed_out, log_totals = attend(joined, live_len)
    (mixed_out,) = meet([mixed_out], meets[0])
    middle = inputs + (dot_plain(mixed_out, qkvo[:, 3 * breadth :]) + parts[4])
    normed_two = layer_norm(middle, parts[5], parts[6]).astype(jnp.bfloat16)
    fore = settled(weights[1])
    pre_act = dot_plain(normed_two, fore) + parts[7]
    activ = gelu_tanh(pre_act).astype(jnp.bfloat16)
    (activ,) = meet([activ], meets[1])
    down = settled(weights[2])
    output = middle + (dot_plain(activ, down) + parts[8])
    return (
        output,
        (inputs, normed, joined, mixed_out, log_totals, middle, normed_two, pre_act, activ),
        (qkvo, fore, down),
    )


def layer_backward(grad_out, saved, weights, vectors, live_len, lead, trees, launch):
    inputs, normed, joined, mixed_out, log_totals, middle, normed_two, pre_act, activ = saved
    qkvo, fore, down = weights
    breadth = inputs.shape[1]
    parts = split_vectors(vectors, breadth, down.shape[0])
    grad_y = grad_out.astype(jnp.bfloat16)
    part_down = core_reduce(activ, grad_y, lead)
    grad_act = dot_outer(grad_y, down)
    grad_pre = jax.vjp(gelu_tanh, pre_act)[1](grad_act)[0].astype(jnp.bfloat16)
    grad_pre, part_down = meet([grad_pre, part_down], trees)
    trees.extend(launch("down", part_down))
    part_fore = core_reduce(normed_two, grad_pre, lead)
    grad_norm_two = dot_outer(grad_pre, fore)
    grad_mid_norm, grad_scale_two, grad_shift_two = jax.vjp(layer_norm, middle, parts[5], parts[6])[
        1
    ](grad_norm_two)
    grad_mid = grad_out + grad_mid_norm
    grad_branch = grad_mid.astype(jnp.bfloat16)
    grad_branch, part_fore = meet([grad_branch, part_fore], trees)
    part_proj = core_reduce(mixed_out, grad_branch, lead)
    grad_mixed = dot_outer(grad_branch, qkvo[:, 3 * breadth :]).astype(jnp.bfloat16)
    grad_mixed, part_proj = meet([grad_mixed, part_proj], trees)
    trees.extend(launch("fore", jnp.concatenate([part_fore, part_proj], 1)))
    grad_joined = attend_back(joined, log_totals, grad_mixed, live_len)
    (grad_joined,) = meet([grad_joined], trees)
    part_qkv = core_reduce(normed, grad_joined, lead)
    grad_normed = dot_outer(grad_joined, qkvo[:, : 3 * breadth])
    grad_in_norm, grad_scale_one, grad_shift_one = jax.vjp(layer_norm, inputs, parts[0], parts[1])[
        1
    ](grad_normed)
    grad_in = grad_mid + grad_in_norm
    grad_in, part_qkv = meet([grad_in, part_qkv], trees)
    joined_sums = jnp.sum(grad_joined.astype(jnp.float32), 0)
    rows = [
        grad_scale_one,
        grad_shift_one,
        joined_sums[:breadth],
        joined_sums[2 * breadth :],
        jnp.sum(grad_branch.astype(jnp.float32), 0),
        grad_scale_two,
        grad_shift_two,
        jnp.sum(grad_pre.astype(jnp.float32), 0),
        jnp.sum(grad_y.astype(jnp.float32), 0),
    ]
    grad_vectors = jnp.concatenate([row.reshape(-1, breadth) for row in rows], 0)
    return (grad_in, grad_vectors, part_qkv)


def adamw(weight, first, second, gradient, rate, decay):
    first_new = 0.5 * first + 0.5 * gradient
    second_new = 0.5 * second + 0.5 * gradient * gradient
    first_hat = first_new / (1.0 - 0.5**STEP)
    second_hat = second_new / (1.0 - 0.5**STEP)
    weight_new = weight - rate * (first_hat / (jnp.sqrt(second_hat) + EPSILON) + decay * weight)
    return (weight_new, first_new, second_new)


FLIP = [(0, 1), (1, 0)]


def across(x, name):
    return lax.ppermute(x, name, FLIP)


def sum_bits(x, names):
    for name in names:
        x = x + across(x, name)
    return x


def per_device(
    shard_names,
    token_ids,
    lengths,
    picked,
    joining,
    embedding,
    embedding_first,
    embedding_second,
    position_table,
    position_first,
    position_second,
    shared_wide,
    shared_wide_first,
    shared_wide_second,
    shared_down,
    shared_down_first,
    shared_down_second,
    shared_vectors,
    shared_vectors_first,
    shared_vectors_second,
    private_wide,
    private_wide_first,
    private_wide_second,
    private_down,
    private_down_first,
    private_down_second,
    private_vectors,
    private_vectors_first,
    private_vectors_second,
):
    half, rest = shard_names[0], shard_names[1:]
    every = ("pair", "core") + shard_names
    crew = ("core",) + rest
    shards = 2 ** len(shard_names)
    clients = 4
    count = clients * shards
    at_pair, at_core, at_half = (lax.axis_index(n) for n in ("pair", "core", half))
    device_at = lax.axis_index(every)
    shard_at = lax.axis_index(shard_names)
    swap_pairs = []
    block = shards // 2
    for pair in range(clients // 2):
        for spot in range(block):
            former = ((pair * 2 + 0) * 2 + 1) * block + spot
            latter = ((pair * 2 + 1) * 2 + 0) * block + spot
            swap_pairs += [(former, latter), (latter, former)]

    seq_len = token_ids.shape[2]
    picks = picked.shape[2]
    slice_rows = embedding.shape[0]

    wide_b = private_wide[0].astype(BF)
    down_b = private_down[0].astype(BF)
    shared_b = shared_wide.astype(BF)
    shared_down_b = shared_down.astype(BF)
    cut = 4 * D

    ids = token_ids[0, 0]
    same = ids[:, None] == ids[None, :]
    at_row = lax.broadcasted_iota(jnp.int32, (seq_len, seq_len), 0)
    at_col = lax.broadcasted_iota(jnp.int32, (seq_len, seq_len), 1)
    first_at = jnp.min(jnp.where(same, at_col, seq_len), 1)
    is_first = first_at == jnp.arange(seq_len, dtype=jnp.int32)
    owners = ids // slice_rows
    slot = jnp.sum(
        (
            (owners[:, None] == owners[None, :]) & is_first[None, :] & (at_col < first_at[:, None])
        ).astype(jnp.int32),
        1,
    )

    vect_own = [shared_vectors, private_vectors[0]]
    pieces = [
        ids.astype(F32),
        slot.astype(F32),
        is_first.astype(F32),
        picked[0, 0].astype(F32),
        lengths[0].astype(F32),
    ] + [v.astype(BF).astype(F32) for v in vect_own]
    starts = [0]
    for piece in pieces:
        starts.append(starts[-1] + piece.shape[0])
    room = max(16, 1024 // count)
    owner_at = jnp.arange(count, dtype=jnp.int32)[:, None, None]
    room_at = jnp.arange(room, dtype=jnp.int32)[None, :, None]
    sought = (owners == owner_at) & (jnp.where(is_first, slot, -1) == room_at)
    sought = jnp.sum(jnp.where(sought, ids - owner_at * slice_rows, 0), 2).astype(F32)
    message = jnp.concatenate(pieces)
    message = jnp.broadcast_to(message, (count,) + message.shape)
    message = jnp.concatenate([message, sought], 1)
    width = message.shape[1]
    message = jnp.pad(message, ((0, 0), (0, -width % 1024))).reshape(count, -1, 128)
    def moved(x):
        return lax.ppermute(x, every, swap_pairs)

    first_moved = moved(wide_b[:, :cut])
    board = lax.all_to_all(message, every, 0, 0, tiled=True).reshape(count, -1)
    posit_b = lax.all_gather(position_table.astype(BF), every, axis=0, tiled=True)[:seq_len]
    posit_names = ("core",) + shard_names
    spread = shard_names + ("pair", "core")
    shared_one = Gather(shared_b[:, :cut], every, spread)
    board, wide_b, down_b, shared_b, shared_down_b = fence(
        board, wide_b, down_b, shared_b, shared_down_b
    )
    (board, first_moved) = meet([board, first_moved], [shared_one])
    stays = at_core == at_half
    there, back = rest + ("core",), rest[::-1] + ("core",)
    private_one = Gather(jnp.where(stays, wide_b[:, :cut], first_moved), crew, there)
    second_moved, third_moved = moved(wide_b[:, cut:]), moved(down_b)

    table_own = embedding.astype(BF)
    pad_rows = -(-slice_rows // 16) * 16
    table_four = Gather(
        jnp.pad(table_own, ((0, pad_rows - slice_rows), (0, 0))),
        ("pair", "core"),
        ("pair", "core"),
        (),
        True,
    )
    filled = jnp.where(
        jnp.arange(clients * pad_rows, dtype=jnp.int32) % pad_rows < slice_rows, 0.0, -jnp.inf
    )

    def posted(place):
        return board[:, starts[place] : starts[place + 1]]

    def hosted(x):
        x = x.reshape((clients // 2, 2, 2, block) + x.shape[1:])
        return jnp.swapaxes(x, 1, 2).reshape((count,) + x.shape[4:])

    all_ids, all_slots, all_first, all_picks, all_lens = [
        hosted(posted(place).astype(jnp.int32)) for place in range(5)
    ]
    vect_s = posted(5).reshape(-1)
    vect_p = lax.dynamic_index_in_dim(
        posted(6).reshape(clients, -1), 2 * at_pair + at_half, 0, False
    )

    all_live = all_picks < all_lens - 1
    live_counts = jnp.sum(all_live.astype(F32), 1).reshape(clients // 2, 2, 2, block)
    counts_all = jnp.sum(live_counts, (1, 3)).reshape(-1)
    joining_f = joining.astype(F32)
    share_all = joining_f / (jnp.sum(joining_f) * counts_all)

    my_ids = lax.dynamic_index_in_dim(all_ids, device_at, 0, False)
    my_slots = lax.dynamic_index_in_dim(all_slots, device_at, 0, False)
    my_picks = lax.dynamic_index_in_dim(all_picks, device_at, 0, False)
    my_len = lax.dynamic_index_in_dim(all_lens, device_at, 0, False)[0]
    my_owners = my_ids // slice_rows

    rounds = jnp.max(all_slots) // room + 1
    in_slice = all_ids - device_at * slice_rows
    wanted = (all_first > 0) & (in_slice >= 0) & (in_slice < slice_rows)

    def asked(turn):
        spots = turn * room + jnp.arange(room, dtype=jnp.int32)
        hits = wanted[:, None, :] & (all_slots[:, None, :] == spots[None, :, None])
        return jnp.sum(jnp.where(hits, in_slice[:, None, :], 0), 2).reshape(-1)

    asked_first = hosted(board[:, width - room : width].astype(jnp.int32)).reshape(-1)

    def land(turn, rows, got):
        spot = my_slots - turn * room
        here = (spot >= 0) & (spot < room)
        found = jnp.take(got, jnp.where(here, my_owners * room + spot, 0), axis=0, mode="clip")
        return jnp.where(here[:, None], found, rows)

    def fetch(turn, rows):
        sent = jnp.take(table_own, asked(turn), axis=0, mode="clip")
        return land(turn, rows, lax.all_to_all(sent, every, 0, 0, tiled=True))

    sent = jnp.take(table_own, asked_first, axis=0, mode="clip")
    (sent,) = meet([sent], [private_one, shared_one])
    got = lax.all_to_all(sent, every, 0, 0, tiled=True)
    shared_two = Gather(shared_b[:, cut:], every, spread)
    shared_three = Gather(shared_down_b, every, spread, (0, 0, 0, 0))
    second_moved, third_moved = meet([second_moved, third_moved], [private_one, shared_one])
    private_two = Gather(jnp.where(stays, wide_b[:, cut:], second_moved), crew, back)
    private_three = Gather(jnp.where(stays, down_b, third_moved), crew, there)
    (got,) = meet([got], [private_two, private_three, shared_two, shared_three])
    rows = land(0, jnp.zeros((seq_len, D), BF), got)
    rows = lax.fori_loop(1, rounds, fetch, rows)
    inputs = rows.astype(F32) + posit_b.astype(F32)

    weights_p = (private_one, private_two, private_three)
    weights_s = (shared_one, shared_two, shared_three)
    first_out, first_saved, weights_p = layer_forward(
        inputs, weights_p, vect_p, my_len, ([private_two, private_three, *weights_s], [shared_two, shared_three])
    )
    second_out, second_saved, weights_s = layer_forward(
        first_out, weights_s, vect_s[: 8 * D + FF], my_len, ([shared_two], [table_four])
    )

    final_scale = vect_s[8 * D + FF : 9 * D + FF]
    final_shift = vect_s[9 * D + FF : 10 * D + FF]
    final_in = jnp.take(second_out, my_picks, axis=0, mode="clip")
    final_b = layer_norm(final_in, final_scale, final_shift).astype(BF)
    target_rows = jnp.take(rows, my_picks + 1, axis=0, mode="clip").astype(F32)

    scored_tree = Gather(final_b, shard_names, shard_names)
    meet([final_b], [scored_tree])
    meet([final_b], [scored_tree, table_four])
    table_four = table_four.result()
    scored = scored_tree.result()

    def group(x):
        x = x.reshape((clients, shards) + x.shape[1:])
        return lax.dynamic_index_in_dim(x, 2 * at_pair + at_core, 0, False)

    group_ids, group_picks, group_live = group(all_ids), group(all_picks), group(all_live)
    seq_at = lax.broadcasted_iota(jnp.int32, (shards, picks, seq_len), 2)
    targets = jnp.sum(
        jnp.where(seq_at == group_picks[:, :, None] + 1, group_ids[:, None, :], 0), 2
    ).reshape(-1)
    host_clients = 2 * at_pair + jnp.arange(shards, dtype=jnp.int32) // block
    weight = jnp.where(group_live, jnp.take(share_all, host_clients)[:, None], 0.0).reshape(-1)
    target_owner = targets // slice_rows
    local_target = jnp.where(
        target_owner % shards == shard_at,
        target_owner // shards * pad_rows + targets % slice_rows,
        -1,
    )
    logits = dot_outer(scored, table_four) + filled
    hit = lax.broadcasted_iota(jnp.int32, logits.shape, 1) == local_target[:, None]
    part_max = jnp.max(logits, -1)
    exponent = jnp.exp(logits - part_max[:, None])
    part_sum = jnp.sum(exponent, -1)
    part_target = jnp.sum(jnp.where(hit, logits, 0.0), -1)
    pulled = dot_plain(exponent.astype(BF), table_four)
    stats = jnp.stack([part_max, part_sum, part_target])
    stats = lax.all_to_all(
        jnp.broadcast_to(stats, (shards,) + stats.shape), shard_names, 0, 0, tiled=True
    )
    pulled, stats = fence(pulled, stats)
    top = jnp.max(stats[:, 0], 0)
    total = jnp.sum(stats[:, 1] * jnp.exp(stats[:, 0] - top), 0)
    target_logit = jnp.sum(stats[:, 2], 0)
    log_all = top + jnp.log(total)
    pulled = (pulled * (weight * jnp.exp(part_max - log_all))[:, None]).astype(BF)
    pulled_tree = Reduce(pulled, shard_names, shard_names[::-1])
    grad_logits = (
        weight[:, None] * jnp.exp(logits - log_all[:, None])
        - jnp.where(hit, weight[:, None], 0.0)
    ).astype(BF)
    head_parts = []
    for part in jnp.split(grad_logits, clients // 2, 1):
        part = dot_inner(part, scored).astype(BF)
        head_parts += meet([part], [pulled_tree])
    pulled_own = pulled_tree.result()

    def own_rows(x):
        return lax.dynamic_slice_in_dim(x, shard_at * picks, picks, 0)

    own_weight = own_rows(weight)
    grad_final_b = pulled_own - own_weight[:, None] * target_rows
    own_live = lax.dynamic_index_in_dim(group_live, shard_at, 0, False)
    own_terms = jnp.sum(jnp.where(own_live, own_rows(log_all - target_logit), 0.0))
    head_trees = [Reduce(part, ("core",), ("core",), None, (1,)) for part in head_parts]

    grad_final_in, grad_fscale, grad_fshift = jax.vjp(
        layer_norm, final_in, final_scale, final_shift
    )[1](grad_final_b)
    grad_second = jnp.zeros_like(second_out).at[my_picks].add(grad_final_in)
    shared_rest, waits_s = ("pair",) + shard_names, {"down": (2,), "fore": (2,), "qkv": (1, 1)}

    def launch_s(kind, part):
        shared_trees[kind] = Reduce(
            part, shared_rest, ("pair",) + shard_names[::-1], None, waits_s[kind]
        )
        return [shared_trees[kind]]

    unswap = (
        lambda x: lax.ppermute(x, every, swap_pairs),
        lambda x, other: jnp.where(at_core == at_half, x, other),
    )
    waits_p = {"down": (2,), "fore": ()}

    def launch_p(kind, part):
        order = rest[::-1] if kind == "down" else rest
        private_trees[kind] = [Reduce(part, rest, order, unswap, waits_p[kind])]
        return private_trees[kind]

    shared_trees, private_trees, trees = {}, {}, list(head_trees)
    grad_first, grad_vect_s, part_qkv = layer_backward(
        grad_second,
        second_saved,
        weights_s,
        vect_s[: 8 * D + FF],
        my_len,
        clients // 2,
        trees,
        launch_s,
    )
    trees.extend(launch_s("qkv", part_qkv))
    head_tree = Reduce(
        jnp.concatenate([tree.result().astype(BF) for tree in head_trees], 0),
        ("pair",),
        ("pair",),
        None,
        (1, 2),
        True,
    )
    trees.append(head_tree)
    vector_s = jnp.concatenate([grad_vect_s, grad_fscale[None], grad_fshift[None]], 0)
    vector_s = vector_s.reshape(count, -1)
    width_s = vector_s.shape[1]
    vector_s = jnp.pad(vector_s, ((0, 0), (0, -width_s % 1024))).reshape(count, -1, 128)
    vector_tree = Exchange(vector_s, every, (0, 2))
    trees.append(vector_tree)
    grad_inputs, grad_vect_p, part_qkv = layer_backward(
        grad_first, first_saved, weights_p, vect_p, my_len, 1, trees, launch_p
    )
    grad_rows = grad_inputs.astype(BF)

    def gathered_up(turn):
        spot = my_slots - turn * room
        here = (spot >= 0) & (spot < room)
        place = jnp.where(here, my_owners * room + spot, -1)
        chosen = lax.broadcasted_iota(jnp.int32, (count * room, seq_len), 0) == place[None, :]
        return dot_plain(chosen.astype(BF), grad_rows).astype(BF)

    def settle(sought, got, total_rows):
        landing = (
            lax.broadcasted_iota(jnp.int32, (slice_rows, count * room), 0) == sought[None, :]
        )
        return total_rows + dot_plain(landing.astype(BF), got)

    def give(turn, total_rows):
        got = lax.all_to_all(gathered_up(turn), every, 0, 0, tiled=True)
        return settle(asked(turn), got, total_rows)

    sent_back = gathered_up(0)

    middle = part_qkv.shape[1] // 2
    sides = grad_vect_p.reshape(2, -1, D)
    keep = lax.dynamic_index_in_dim(sides, at_core, 0, False)
    keep = keep + across(lax.dynamic_index_in_dim(sides, 1 - at_core, 0, False), "core")
    keep = keep.astype(BF).reshape(block, 1, -1)
    width_p = keep.shape[2]
    keep = jnp.pad(keep, ((0, 0), (0, 15), (0, middle - width_p)))
    qkv_one = part_qkv[:, :middle].reshape(block, -1, middle)
    height = qkv_one.shape[1]
    qkv_one = jnp.concatenate([qkv_one, keep], 1).reshape(-1, middle)
    tree_one = Reduce(qkv_one, rest, rest[::-1], unswap)
    tree_two = Reduce(part_qkv[:, middle:], rest, rest, unswap)
    trees += [tree_one, tree_two]
    (sent_back,) = meet([sent_back], trees)
    got_back = lax.all_to_all(sent_back, every, 0, 0, tiled=True)

    posit_tree = Reduce(grad_rows, posit_names, ("core",) + shard_names[::-1])
    meet([sent_back], trees + [posit_tree])
    meet([sent_back], [posit_tree])
    grad_posit = posit_tree.result()
    grad_posit = grad_posit + across(grad_posit.astype(BF), "pair").astype(F32)
    grad_posit = jnp.where(at_pair == 0, grad_posit, 0.0)
    grad_vect_sh = jnp.sum(vector_tree.result().reshape(count, -1), 0)[:width_s]
    head_own = head_tree.result()[:slice_rows]
    g_down_s, g_fore_s, g_qkv_s = [
        shared_trees[kind].result() for kind in ("down", "fore", "qkv")
    ]
    g_wide_s = jnp.concatenate([g_qkv_s, g_fore_s[:, FF:], g_fore_s[:, :FF]], 1)
    g_down_p, g_fore_p = [private_trees[kind][0].result() for kind in ("down", "fore")]
    g_qkv_p, g_qkv_q = tree_one.result(), tree_two.result()
    g_qkv_p, grad_vect_ph = g_qkv_p[:height], g_qkv_p[height, :width_p]
    g_wide_p = jnp.concatenate([g_qkv_p, g_qkv_q, g_fore_p[:, FF:], g_fore_p[:, :FF]], 1)

    grad_table = settle(asked_first, got_back, head_own)
    grad_table = lax.fori_loop(1, rounds, give, grad_table)

    all_grads = [
        grad_table,
        grad_posit,
        g_wide_s,
        g_down_s,
        grad_vect_sh,
        g_wide_p[None],
        g_down_p[None],
        grad_vect_ph[None],
    ]
    squares = jnp.zeros((), jnp.float32)
    for gradient in all_grads:
        squares = squares + jnp.sum(gradient * gradient)
    client_at = jnp.arange(clients, dtype=jnp.int32)
    loss_vector = jnp.where(client_at == 2 * at_pair + at_half, own_terms, 0.0)
    figures = jnp.pad(jnp.concatenate([squares[None], loss_vector]), (0, 127 - clients))
    figures = sum_bits(figures, every)
    grad_norm = jnp.sqrt(figures[0])
    own_client = client_at == 2 * at_pair + at_core
    loss_sum = jnp.sum(jnp.where(own_client, figures[1 : 1 + clients], 0.0))
    count_sum = jnp.sum(jnp.where(own_client, counts_all, 0.0))
    factor = jnp.minimum(1.0, CLIP_NORM / grad_norm)
    g_table, g_posit, g_wide_s, g_down_s, g_vect_s, g_wide_p, g_down_p, g_vect_p = [
        member * factor for member in all_grads
    ]
    results = []
    for state, gradient, rate, decay in (
        ((embedding, embedding_first, embedding_second), g_table, RATE_MATRIX, DECAY),
        ((position_table, position_first, position_second), g_posit, RATE_MATRIX, DECAY),
        ((shared_wide, shared_wide_first, shared_wide_second), g_wide_s, RATE_MATRIX, DECAY),
        ((shared_down, shared_down_first, shared_down_second), g_down_s, RATE_MATRIX, DECAY),
        ((shared_vectors, shared_vectors_first, shared_vectors_second), g_vect_s, RATE_VECTOR, 0.0),
        ((private_wide, private_wide_first, private_wide_second), g_wide_p, RATE_MATRIX, DECAY),
        ((private_down, private_down_first, private_down_second), g_down_p, RATE_MATRIX, DECAY),
        (
            (private_vectors, private_vectors_first, private_vectors_second),
            g_vect_p,
            RATE_VECTOR,
            0.0,
        ),
    ):
        results += adamw(*state, gradient, rate, decay)
    return (*results, loss_sum.reshape(1), count_sum.reshape(1), grad_norm)


def solution(mesh):
    clients, shards = mesh.shape["client"], mesh.shape["shard"]
    depth = shards.bit_length() - 1
    if clients != 4 or shards != 2**depth:
        raise ValueError("mesh sizes")
    shard_names = tuple("s%d" % place for place in range(depth))
    fine = Mesh(
        mesh.devices.reshape((clients // 2, 2) + (2,) * depth), ("pair", "core") + shard_names
    )
    client, shard, both = ("pair", "core"), shard_names, ("pair", "core") + shard_names
    table, block, vector, lot = P(both, None), P(client, shard, None), P(both), P(client, shard)
    in_specs = (
        (block, lot, block, P())
        + (table,) * 12
        + (vector,) * 3
        + (block,) * 6
        + (lot,) * 3
    )
    out_specs = (
        (table,) * 12 + (vector,) * 3 + (block,) * 6 + (lot,) * 3 + (P(client), P(client), P())
    )

    def run(*arrays):
        return per_device(shard_names, *arrays)

    return jax.shard_map(
        run, mesh=fine, in_specs=in_specs, out_specs=out_specs, check_vma=False
    )
```

```python
import jax
import jax.numpy as jnp
from jax import lax
from jax.experimental import pallas as pl
from jax.experimental.pallas import tpu as pltpu
from jax.sharding import Mesh
from jax.sharding import PartitionSpec as P

HD = 64
D = 768
FF = 3072
NPOS = 1024
STEP = 5


SCALE = 0.125
CLIP_NORM = 0.01
RATE_MATRIX = 0.03
RATE_VECTOR = 0.5
DECAY = 0.01
EPSILON = 1e-08
BF = jnp.bfloat16
F32 = jnp.float32
NT = (((1,), (1,)), ((), ()))
TN = (((0,), (0,)), ((), ()))


def dot_plain(former, latter):
    return jnp.dot(former, latter, preferred_element_type=jnp.float32)


def dot_inner(former, latter):
    return lax.dot_general(
        former, latter, (((0,), (0,)), ((), ())), preferred_element_type=jnp.float32
    )


def dot_outer(former, latter):
    return lax.dot_general(
        former, latter, (((1,), (1,)), ((), ())), preferred_element_type=jnp.float32
    )


def layer_norm(values, scales, shifts):
    centre = values - jnp.mean(values, -1, keepdims=True)
    spread = jnp.mean(centre * centre, -1, keepdims=True)
    return centre * lax.rsqrt(spread + 1e-05) * scales + shifts


def gelu_tanh(values):
    return jax.nn.gelu(values, approximate=True)


def split_vectors(vectors, breadth, hidden):
    starts = [
        0,
        breadth,
        2 * breadth,
        3 * breadth,
        4 * breadth,
        5 * breadth,
        6 * breadth,
        7 * breadth,
        7 * breadth + hidden,
        8 * breadth + hidden,
    ]
    return [vectors[starts[position] : starts[position + 1]] for position in range(9)]


def product(former, latter, form):
    return lax.dot_general(former, latter, form, preferred_element_type=F32)


def write_mask(live_ref, mask_ref):
    keys = lax.broadcasted_iota(jnp.int32, mask_ref.shape, 0)
    queries = lax.broadcasted_iota(jnp.int32, mask_ref.shape, 1)
    allowed = (keys <= queries) & (keys < live_ref[0])
    mask_ref[...] = jnp.where(allowed, 0.0, -1e30)


def attend_kernel(live_ref, q_ref, k_ref, v_ref, out_ref, log_ref, mask_ref):
    @pl.when(pl.program_id(0) == 0)
    def _():
        write_mask(live_ref, mask_ref)

    tokens, width = q_ref.shape
    tile = tokens // 2
    for head in range(width // HD):
        cols = slice(head * HD, (head + 1) * HD)
        queries, keys, values = q_ref[:, cols] * SCALE, k_ref[:, cols], v_ref[:, cols]
        for part in range(2):
            begin, end = part * tile, (part + 1) * tile
            scores = product(keys[:end], queries[begin:end], NT) + mask_ref[:end, begin:end]
            highest = jnp.max(scores, 0, keepdims=True)
            exponent = jnp.exp(scores - highest)
            total = jnp.sum(exponent, 0, keepdims=True)
            probs = (exponent * (1.0 / total)).astype(BF)
            mixed = product(values[:end], probs, TN)
            out_ref[begin:end, cols] = mixed.T.astype(BF)
            log_ref[0, head : head + 1, begin:end] = highest + jnp.log(total)


def attend_back_kernel(live_ref, q_ref, k_ref, v_ref, grad_ref, log_ref, out_ref, mask_ref):
    @pl.when(pl.program_id(0) == 0)
    def _():
        write_mask(live_ref, mask_ref)

    tokens, width = q_ref.shape
    tile = tokens // 2
    breadth = out_ref.shape[1] // 3
    sides = [[], [], []]
    for head in range(width // HD):
        cols = slice(head * HD, (head + 1) * HD)
        queries, keys, values = q_ref[:, cols] * SCALE, k_ref[:, cols], v_ref[:, cols]
        grads = grad_ref[:, cols]
        grad_queries, grad_keys, grad_values = [], [], []
        for part in range(2):
            begin, end = part * tile, (part + 1) * tile
            scores = product(keys[:end], queries[begin:end], NT) + mask_ref[:end, begin:end]
            probs = jnp.exp(scores - log_ref[0, head : head + 1, begin:end])
            grad_out = grads[begin:end]
            grad_values.append(
                jnp.dot(probs.astype(BF), grad_out, preferred_element_type=F32)
            )
            grad_probs = product(values[:end], grad_out, NT)
            inner = jnp.sum(grad_probs * probs, 0, keepdims=True)
            grad_scores = (probs * (grad_probs - inner)).astype(BF)
            grad_keys.append(
                jnp.dot(grad_scores, queries[begin:end], preferred_element_type=F32)
            )
            grad_queries.append(product(keys[:end], grad_scores, TN).T * SCALE)
        for side, parts in ((1, grad_keys), (2, grad_values)):
            sides[side].append(
                jnp.concatenate([parts[0] + parts[1][:tile], parts[1][tile:]], 0)
            )
        sides[0].append(jnp.concatenate(grad_queries, 0))
    place = pl.program_id(0) * width
    for side in range(3):
        start = pl.multiple_of(side * breadth + place, width)
        out_ref[:, pl.ds(start, width)] = jnp.concatenate(sides[side], 1).astype(BF)


def attend(joined, live_len):
    tokens, breadth = joined.shape[0], joined.shape[1] // 3
    width = 2 * HD
    pairs = breadth // width
    parts = [
        pl.BlockSpec((tokens, width), lambda i, n, side=side: (0, side * pairs + i))
        for side in range(3)
    ]
    return pl.pallas_call(
        attend_kernel,
        grid_spec=pltpu.PrefetchScalarGridSpec(
            num_scalar_prefetch=1,
            grid=(pairs,),
            in_specs=parts,
            out_specs=[
                pl.BlockSpec((tokens, width), lambda i, n: (0, i)),
                pl.BlockSpec((1, 2, tokens), lambda i, n: (i, 0, 0)),
            ],
            scratch_shapes=[pltpu.VMEM((tokens, tokens), F32)],
        ),
        out_shape=[
            jax.ShapeDtypeStruct((tokens, breadth), BF),
            jax.ShapeDtypeStruct((pairs, 2, tokens), F32),
        ],
        compiler_params=pltpu.CompilerParams(vmem_limit_bytes=32 << 20),
        cost_estimate=pl.CostEstimate(flops=0, bytes_accessed=0, transcendentals=0),
    )(live_len.reshape(1), joined, joined, joined)


def attend_back(joined, log_total, grad_mixed, live_len):
    tokens, breadth = grad_mixed.shape
    width = 2 * HD
    pairs = breadth // width
    parts = [
        pl.BlockSpec((tokens, width), lambda i, n, side=side: (0, side * pairs + i))
        for side in range(3)
    ]
    return pl.pallas_call(
        attend_back_kernel,
        grid_spec=pltpu.PrefetchScalarGridSpec(
            num_scalar_prefetch=1,
            grid=(pairs,),
            in_specs=parts
            + [
                pl.BlockSpec((tokens, width), lambda i, n: (0, i)),
                pl.BlockSpec((1, 2, tokens), lambda i, n: (i, 0, 0)),
            ],
            out_specs=pl.BlockSpec((tokens, 3 * breadth), lambda i, n: (0, 0)),
            scratch_shapes=[pltpu.VMEM((tokens, tokens), F32)],
        ),
        out_shape=jax.ShapeDtypeStruct((tokens, 3 * breadth), BF),
        compiler_params=pltpu.CompilerParams(vmem_limit_bytes=32 << 20),
        cost_estimate=pl.CostEstimate(flops=0, bytes_accessed=0, transcendentals=0),
    )(live_len.reshape(1), joined, joined, joined, grad_mixed, log_total)


def fence(*arrays):
    return lax.optimization_barrier(arrays)


class Tree:
    def tied(self):
        return [self.held] if self.other is None else [self.held, self.other]

    def retie(self, arrays):
        self.held = arrays[0]
        if self.other is not None:
            self.other = arrays[1]

    def step(self):
        if self.other is None:
            self.send()
        else:
            self.advance()

    def result(self):
        while self.open:
            self.step()
        return self.final()


class Gather(Tree):
    def __init__(self, block, names, order, waits=(), lazy=False):
        self.names, self.order, self.rows, self.waits = names, list(order), block.shape, list(waits)
        self.held = block.reshape((1,) * len(names) + block.shape)
        self.other = None
        if not lazy:
            self.send()

    def send(self):
        self.other = across(self.held, self.order[0])

    def advance(self):
        name = self.order.pop(0)
        dim, low_side = self.names.index(name), lax.axis_index(name) == 0
        self.held = jnp.where(
            low_side,
            jnp.concatenate([self.held, self.other], dim),
            jnp.concatenate([self.other, self.held], dim),
        )
        self.other = None
        if self.order:
            self.send()

    @property
    def open(self):
        return bool(self.order)

    def final(self):
        return self.held.reshape((-1,) + self.rows[1:])


class Reduce(Tree):
    def __init__(self, blocks, names, order, after=None, waits=(), lazy=False):
        self.names, self.order, self.after, self.waits = names, list(order), after, list(waits)
        self.tail = blocks.shape[1:]
        self.held = blocks.reshape((2,) * len(names) + (-1,) + self.tail)
        self.other = None
        if not lazy:
            self.send()

    def send(self):
        if self.order:
            name = self.order[0]
            dim, side = self.names.index(name), lax.axis_index(name)
            self.other = across(lax.dynamic_index_in_dim(self.held, 1 - side, dim, True), name)
            self.held = lax.dynamic_index_in_dim(self.held, side, dim, True)
        else:
            self.held = self.held.astype(BF)
            self.other = self.after[0](self.held)

    def advance(self):
        if self.order:
            self.order.pop(0)
            total = self.held.astype(F32) + self.other.astype(F32)
            self.held = total.astype(BF) if self.order else total
        else:
            self.held = self.after[1](self.held, self.other)
            self.after = None
        self.other = None
        if self.open:
            self.send()

    @property
    def open(self):
        return bool(self.order) or self.after is not None

    def final(self):
        return self.held.astype(F32).reshape((-1,) + self.tail)


class Exchange(Tree):
    def __init__(self, packet, names, waits):
        self.held, self.names, self.waits = packet, names, list(waits)
        self.other, self.open = None, True

    def send(self):
        self.other = lax.all_to_all(self.held, self.names, 0, 0, tiled=True)

    def advance(self):
        self.open = False

    def final(self):
        return self.other


def meet(carry, trees):
    due = []
    for tree in trees:
        if tree.open:
            if tree.waits and tree.waits[0] > 0:
                tree.waits[0] -= 1
            else:
                tree.waits = tree.waits[1:]
                due.append(tree)
    flat, spans = list(carry), []
    for tree in due:
        start = len(flat)
        flat += tree.tied()
        spans.append((start, len(flat)))
    flat = fence(*flat)
    for tree, (start, stop) in zip(due, spans):
        tree.retie(flat[start:stop])
        tree.step()
    return flat[: len(carry)]


def core_half(active, lead, side):
    width = active.shape[1] // (2 * lead)
    if width % 128:
        pieces = [
            active[:, (2 * part + core) * width : (2 * part + core + 1) * width]
            for core in range(2)
            for part in range(lead)
        ]
        active, lead, width = jnp.concatenate(pieces, 1), 1, width * lead
    pieces = [
        lax.dynamic_slice_in_dim(active, (2 * part + side) * width, width, 1)
        for part in range(lead)
    ]
    return pieces[0] if lead == 1 else jnp.concatenate(pieces, 1)


def core_reduce(active, grad, lead):
    side = lax.axis_index("core")
    send = dot_inner(core_half(active, lead, 1 - side), grad).astype(BF)
    other = across(send, "core")
    return (dot_inner(core_half(active, lead, side), grad) + other.astype(F32)).astype(BF)


def settled(weight):
    return weight.result() if isinstance(weight, Tree) else weight


def layer_forward(inputs, weights, vectors, live_len, meets):
    breadth = inputs.shape[1]
    parts = split_vectors(vectors, breadth, vectors.shape[0] - 8 * breadth)
    normed = layer_norm(inputs, parts[0], parts[1]).astype(jnp.bfloat16)
    shift_qkv = jnp.concatenate([parts[2], jnp.zeros_like(parts[2]), parts[3]])
    qkvo = settled(weights[0])
    joined = (dot_plain(normed, qkvo[:, : 3 * breadth]) + shift_qkv).astype(jnp.bfloat16)
    mixed_out, log_totals = attend(joined, live_len)
    (mixed_out,) = meet([mixed_out], meets[0])
    middle = inputs + (dot_plain(mixed_out, qkvo[:, 3 * breadth :]) + parts[4])
    normed_two = layer_norm(middle, parts[5], parts[6]).astype(jnp.bfloat16)
    fore = settled(weights[1])
    pre_act = dot_plain(normed_two, fore) + parts[7]
    activ = gelu_tanh(pre_act).astype(jnp.bfloat16)
    (activ,) = meet([activ], meets[1])
    down = settled(weights[2])
    output = middle + (dot_plain(activ, down) + parts[8])
    return (
        output,
        (inputs, normed, joined, mixed_out, log_totals, middle, normed_two, pre_act, activ),
        (qkvo, fore, down),
    )


def layer_backward(grad_out, saved, weights, vectors, live_len, lead, trees, launch):
    inputs, normed, joined, mixed_out, log_totals, middle, normed_two, pre_act, activ = saved
    qkvo, fore, down = weights
    breadth = inputs.shape[1]
    parts = split_vectors(vectors, breadth, down.shape[0])
    grad_y = grad_out.astype(jnp.bfloat16)
    part_down = core_reduce(activ, grad_y, lead)
    grad_act = dot_outer(grad_y, down)
    grad_pre = jax.vjp(gelu_tanh, pre_act)[1](grad_act)[0].astype(jnp.bfloat16)
    grad_pre, part_down = meet([grad_pre, part_down], trees)
    trees.extend(launch("down", part_down))
    part_fore = core_reduce(normed_two, grad_pre, lead)
    grad_norm_two = dot_outer(grad_pre, fore)
    grad_mid_norm, grad_scale_two, grad_shift_two = jax.vjp(layer_norm, middle, parts[5], parts[6])[
        1
    ](grad_norm_two)
    grad_mid = grad_out + grad_mid_norm
    grad_branch = grad_mid.astype(jnp.bfloat16)
    grad_branch, part_fore = meet([grad_branch, part_fore], trees)
    part_proj = core_reduce(mixed_out, grad_branch, lead)
    grad_mixed = dot_outer(grad_branch, qkvo[:, 3 * breadth :]).astype(jnp.bfloat16)
    grad_mixed, part_proj = meet([grad_mixed, part_proj], trees)
    trees.extend(launch("fore", (part_fore, part_proj)))
    grad_joined = attend_back(joined, log_totals, grad_mixed, live_len)
    (grad_joined,) = meet([grad_joined], trees)
    part_qkv = core_reduce(normed, grad_joined, lead)
    grad_normed = dot_outer(grad_joined, qkvo[:, : 3 * breadth])
    (grad_normed,) = meet([grad_normed], trees if lead == 1 else [])
    grad_in_norm, grad_scale_one, grad_shift_one = jax.vjp(layer_norm, inputs, parts[0], parts[1])[
        1
    ](grad_normed)
    grad_in = grad_mid + grad_in_norm
    grad_in, part_qkv = meet([grad_in, part_qkv], trees)
    joined_sums = jnp.sum(grad_joined.astype(jnp.float32), 0)
    rows = [
        grad_scale_one,
        grad_shift_one,
        joined_sums[:breadth],
        joined_sums[2 * breadth :],
        jnp.sum(grad_branch.astype(jnp.float32), 0),
        grad_scale_two,
        grad_shift_two,
        jnp.sum(grad_pre.astype(jnp.float32), 0),
        jnp.sum(grad_y.astype(jnp.float32), 0),
    ]
    grad_vectors = jnp.concatenate([row.reshape(-1, breadth) for row in rows], 0)
    return (grad_in, grad_vectors, part_qkv)


def adamw(weight, first, second, gradient, rate, decay):
    first_new = 0.5 * first + 0.5 * gradient
    second_new = 0.5 * second + 0.5 * gradient * gradient
    first_hat = first_new / (1.0 - 0.5**STEP)
    second_hat = second_new / (1.0 - 0.5**STEP)
    weight_new = weight - rate * (first_hat / (jnp.sqrt(second_hat) + EPSILON) + decay * weight)
    return (weight_new, first_new, second_new)


FLIP = [(0, 1), (1, 0)]


def across(x, name):
    return lax.ppermute(x, name, FLIP)


def per_device(
    shard_names,
    token_ids,
    lengths,
    picked,
    joining,
    embedding,
    embedding_first,
    embedding_second,
    position_table,
    position_first,
    position_second,
    shared_wide,
    shared_wide_first,
    shared_wide_second,
    shared_down,
    shared_down_first,
    shared_down_second,
    shared_vectors,
    shared_vectors_first,
    shared_vectors_second,
    private_wide,
    private_wide_first,
    private_wide_second,
    private_down,
    private_down_first,
    private_down_second,
    private_vectors,
    private_vectors_first,
    private_vectors_second,
):
    half, rest = shard_names[0], shard_names[1:]
    every = ("pair", "core") + shard_names
    crew = ("core",) + rest
    shards = 2 ** len(shard_names)
    clients = 4
    count = clients * shards
    at_pair, at_core, at_half = (lax.axis_index(n) for n in ("pair", "core", half))
    device_at = lax.axis_index(every)
    shard_at = lax.axis_index(shard_names)
    swap_pairs = []
    block = shards // 2
    for pair in range(clients // 2):
        for spot in range(block):
            former = ((pair * 2 + 0) * 2 + 1) * block + spot
            latter = ((pair * 2 + 1) * 2 + 0) * block + spot
            swap_pairs += [(former, latter), (latter, former)]

    seq_len = token_ids.shape[2]
    picks = picked.shape[2]
    slice_rows = embedding.shape[0]

    wide_b = private_wide[0].astype(BF)
    down_b = private_down[0].astype(BF)
    shared_b = shared_wide.astype(BF)
    shared_down_b = shared_down.astype(BF)
    cut = 4 * D

    ids = token_ids[0, 0]
    same = ids[:, None] == ids[None, :]
    at_row = lax.broadcasted_iota(jnp.int32, (seq_len, seq_len), 0)
    at_col = lax.broadcasted_iota(jnp.int32, (seq_len, seq_len), 1)
    first_at = jnp.min(jnp.where(same, at_col, seq_len), 1)
    is_first = first_at == jnp.arange(seq_len, dtype=jnp.int32)
    owners = ids // slice_rows
    slot = jnp.sum(
        (
            (owners[:, None] == owners[None, :]) & is_first[None, :] & (at_col < first_at[:, None])
        ).astype(jnp.int32),
        1,
    )

    vect_own = [shared_vectors, private_vectors[0]]
    pieces = [
        ids.astype(F32),
        slot.astype(F32),
        is_first.astype(F32),
        picked[0, 0].astype(F32),
        lengths[0].astype(F32),
    ] + [v.astype(BF).astype(F32) for v in vect_own]
    starts = [0]
    for piece in pieces:
        starts.append(starts[-1] + piece.shape[0])
    room = max(16, 1024 // count)
    owner_at = jnp.arange(count, dtype=jnp.int32)[:, None, None]
    room_at = jnp.arange(room, dtype=jnp.int32)[None, :, None]
    sought = (owners == owner_at) & (jnp.where(is_first, slot, -1) == room_at)
    sought = jnp.sum(jnp.where(sought, ids - owner_at * slice_rows, 0), 2).astype(F32)
    message = jnp.concatenate(pieces)
    message = jnp.broadcast_to(message, (count,) + message.shape)
    message = jnp.concatenate([message, sought], 1)
    width = message.shape[1]
    message = jnp.pad(message, ((0, 0), (0, -width % 1024))).reshape(count, -1, 128)
    first_moved = lax.ppermute(wide_b[:, :cut], every, swap_pairs)
    table_own = embedding.astype(BF)
    pad_rows = -(-slice_rows // 16) * 16
    table_four = Gather(
        jnp.pad(table_own, ((0, pad_rows - slice_rows), (0, 0))),
        ("pair", "core"),
        ("pair", "core"),
    )
    def moved(x):
        return lax.ppermute(x, every, swap_pairs)

    board = lax.all_to_all(message, every, 0, 0, tiled=True).reshape(count, -1)
    posit_b = lax.all_gather(position_table.astype(BF), every, axis=0, tiled=True)[:seq_len]
    posit_names = ("core",) + shard_names
    spread = shard_names + ("pair", "core")
    shared_one = Gather(shared_b[:, :cut], every, spread)
    board, wide_b, down_b, shared_b, shared_down_b = fence(
        board, wide_b, down_b, shared_b, shared_down_b
    )
    (board, first_moved) = meet([board, first_moved], [shared_one])
    stays = at_core == at_half
    there, back = rest + ("core",), rest[::-1] + ("core",)
    private_one = Gather(jnp.where(stays, wide_b[:, :cut], first_moved), crew, back)
    second_moved, third_moved = moved(wide_b[:, cut:]), moved(down_b)

    filled = jnp.where(
        jnp.arange(clients * pad_rows, dtype=jnp.int32) % pad_rows < slice_rows, 0.0, -jnp.inf
    )

    def posted(place):
        return board[:, starts[place] : starts[place + 1]]

    def hosted(x):
        x = x.reshape((clients // 2, 2, 2, block) + x.shape[1:])
        return jnp.swapaxes(x, 1, 2).reshape((count,) + x.shape[4:])

    all_ids, all_slots, all_first, all_picks, all_lens = [
        hosted(posted(place).astype(jnp.int32)) for place in range(5)
    ]
    vect_s = posted(5).reshape(-1)
    vect_p = lax.dynamic_index_in_dim(
        posted(6).reshape(clients, -1), 2 * at_pair + at_half, 0, False
    )

    all_live = all_picks < all_lens - 1
    live_counts = jnp.sum(all_live.astype(F32), 1).reshape(clients // 2, 2, 2, block)
    counts_all = jnp.sum(live_counts, (1, 3)).reshape(-1)
    joining_f = joining.astype(F32)
    share_all = joining_f / (jnp.sum(joining_f) * counts_all)

    my_ids = lax.dynamic_index_in_dim(all_ids, device_at, 0, False)
    my_slots = lax.dynamic_index_in_dim(all_slots, device_at, 0, False)
    my_picks = lax.dynamic_index_in_dim(all_picks, device_at, 0, False)
    my_len = lax.dynamic_index_in_dim(all_lens, device_at, 0, False)[0]
    my_owners = my_ids // slice_rows

    rounds = jnp.max(all_slots) // room + 1
    in_slice = all_ids - device_at * slice_rows
    wanted = (all_first > 0) & (in_slice >= 0) & (in_slice < slice_rows)

    def asked(turn):
        spots = turn * room + jnp.arange(room, dtype=jnp.int32)
        hits = wanted[:, None, :] & (all_slots[:, None, :] == spots[None, :, None])
        return jnp.sum(jnp.where(hits, in_slice[:, None, :], 0), 2).reshape(-1)

    asked_first = hosted(board[:, width - room : width].astype(jnp.int32)).reshape(-1)

    def land(turn, rows, got):
        spot = my_slots - turn * room
        here = (spot >= 0) & (spot < room)
        found = jnp.take(got, jnp.where(here, my_owners * room + spot, 0), axis=0, mode="clip")
        return jnp.where(here[:, None], found, rows)

    def fetch(turn, rows):
        sent = jnp.take(table_own, asked(turn), axis=0, mode="clip")
        return land(turn, rows, lax.all_to_all(sent, every, 0, 0, tiled=True))

    sent = jnp.take(table_own, asked_first, axis=0, mode="clip")
    got = lax.all_to_all(sent, every, 0, 0, tiled=True)
    shared_two = Gather(shared_b[:, cut:], every, spread)
    shared_three = Gather(shared_down_b, every, spread)
    second_moved, third_moved = meet([second_moved, third_moved], [private_one, shared_one])
    private_two = Gather(jnp.where(stays, wide_b[:, cut:], second_moved), crew, back)
    private_three = Gather(jnp.where(stays, down_b, third_moved), crew, there)
    meet([], [shared_one])
    meet([], [private_one, private_two, private_three, shared_two, shared_three])
    meet([], [shared_two, shared_three])
    (got,) = meet([got], [table_four])
    rows = land(0, jnp.zeros((seq_len, D), BF), got)
    rows = lax.fori_loop(1, rounds, fetch, rows)
    inputs = rows.astype(F32) + posit_b.astype(F32)

    weights_p = (private_one, private_two, private_three)
    weights_s = (shared_one, shared_two, shared_three)
    first_out, first_saved, weights_p = layer_forward(
        inputs, weights_p, vect_p, my_len, ([private_two, private_three, shared_one, shared_two], [shared_three])
    )
    second_out, second_saved, weights_s = layer_forward(
        first_out, weights_s, vect_s[: 8 * D + FF], my_len, ([shared_two], [])
    )

    final_scale = vect_s[8 * D + FF : 9 * D + FF]
    final_shift = vect_s[9 * D + FF : 10 * D + FF]
    final_in = jnp.take(second_out, my_picks, axis=0, mode="clip")
    final_b = layer_norm(final_in, final_scale, final_shift).astype(BF)
    target_rows = jnp.take(rows, my_picks + 1, axis=0, mode="clip").astype(F32)

    scored_tree = Gather(final_b, shard_names, shard_names)
    meet([final_b], [scored_tree])
    table_four = table_four.result()
    scored = scored_tree.result()

    def group(x):
        x = x.reshape((clients, shards) + x.shape[1:])
        return lax.dynamic_index_in_dim(x, 2 * at_pair + at_core, 0, False)

    group_ids, group_picks, group_live = group(all_ids), group(all_picks), group(all_live)
    seq_at = lax.broadcasted_iota(jnp.int32, (shards, picks, seq_len), 2)
    targets = jnp.sum(
        jnp.where(seq_at == group_picks[:, :, None] + 1, group_ids[:, None, :], 0), 2
    ).reshape(-1)
    host_clients = 2 * at_pair + jnp.arange(shards, dtype=jnp.int32) // block
    weight = jnp.where(group_live, jnp.take(share_all, host_clients)[:, None], 0.0).reshape(-1)
    target_owner = targets // slice_rows
    local_target = jnp.where(
        target_owner % shards == shard_at,
        target_owner // shards * pad_rows + targets % slice_rows,
        -1,
    )
    logits = dot_outer(scored, table_four) + filled
    hit = lax.broadcasted_iota(jnp.int32, logits.shape, 1) == local_target[:, None]
    part_max = jnp.max(logits, -1)
    exponent = jnp.exp(logits - part_max[:, None])
    part_sum = jnp.sum(exponent, -1)
    part_target = jnp.sum(jnp.where(hit, logits, 0.0), -1)
    exponent, part_sum, part_target = fence(exponent.astype(BF), part_sum, part_target)
    pulled = dot_plain(exponent, table_four)
    stats = jnp.stack([part_max, part_sum, part_target])
    stats = lax.all_to_all(
        jnp.broadcast_to(stats, (shards,) + stats.shape), shard_names, 0, 0, tiled=True
    )
    pulled, stats = fence(pulled, stats)
    top = jnp.max(stats[:, 0], 0)
    total = jnp.sum(stats[:, 1] * jnp.exp(stats[:, 0] - top), 0)
    target_logit = jnp.sum(stats[:, 2], 0)
    log_all = top + jnp.log(total)
    pulled = (pulled * (weight * jnp.exp(part_max - log_all))[:, None]).astype(BF)
    pulled_tree = Reduce(pulled, shard_names, shard_names[::-1])
    grad_logits = (
        exponent.astype(F32) * (weight * jnp.exp(part_max - log_all))[:, None]
        - jnp.where(hit, weight[:, None], 0.0)
    ).astype(BF)
    head_parts = []
    for part in jnp.split(grad_logits, clients // 2, 1):
        part = dot_inner(part, scored).astype(BF)
        head_parts += meet([part], [pulled_tree])
    pulled_own = pulled_tree.result()

    def own_rows(x):
        return lax.dynamic_slice_in_dim(x, shard_at * picks, picks, 0)

    own_weight = own_rows(weight)
    grad_final_b = pulled_own - own_weight[:, None] * target_rows
    own_live = lax.dynamic_index_in_dim(group_live, shard_at, 0, False)
    own_terms = jnp.sum(jnp.where(own_live, own_rows(log_all - target_logit), 0.0))
    head_trees = [Reduce(part, ("core",), ("core",), None, (1,)) for part in head_parts]

    grad_final_in, grad_fscale, grad_fshift = jax.vjp(
        layer_norm, final_in, final_scale, final_shift
    )[1](grad_final_b)
    grad_second = jnp.zeros_like(second_out).at[my_picks].add(grad_final_in)
    shared_rest = ("pair",) + shard_names

    def launch_s(kind, part):
        if kind == "fore":
            shared_trees[kind] = part
            return []
        if kind == "qkv":
            part = jnp.concatenate([part, *shared_trees["fore"][::-1]], 1)
        waits = (2,) if kind == "down" else (3, 1)
        shared_trees[kind] = Reduce(
            part, shared_rest, ("pair",) + shard_names[::-1], None, waits
        )
        return [shared_trees[kind]]

    unswap = (
        lambda x: lax.ppermute(x, every, swap_pairs),
        lambda x, other: jnp.where(at_core == at_half, x, other),
    )
    waits_p = {"down": (2,), "fore": (1,)}

    def launch_p(kind, part):
        order = rest[::-1] if kind == "down" else rest
        if kind == "fore":
            part = jnp.concatenate(part, 1)
        private_trees[kind] = [Reduce(part, rest, order, unswap, waits_p[kind])]
        return private_trees[kind]

    shared_trees, private_trees, trees = {}, {}, list(head_trees)
    grad_first, grad_vect_s, part_qkv = layer_backward(
        grad_second,
        second_saved,
        weights_s,
        vect_s[: 8 * D + FF],
        my_len,
        clients // 2,
        trees,
        launch_s,
    )
    trees.extend(launch_s("qkv", part_qkv))
    head_tree = Reduce(
        jnp.concatenate([tree.result().astype(BF) for tree in head_trees], 0),
        ("pair",),
        ("pair",),
        None,
        (3, 2),
        True,
    )
    trees.append(head_tree)
    vector_s = jnp.concatenate([grad_vect_s, grad_fscale[None], grad_fshift[None]], 0)
    vector_s = vector_s.reshape(count, -1)
    width_s = vector_s.shape[1]
    vector_s = jnp.pad(vector_s, ((0, 0), (0, -width_s % 1024))).reshape(count, -1, 128)
    vector_tree = Exchange(vector_s, every, (0, 2))
    trees.append(vector_tree)
    grad_inputs, grad_vect_p, part_qkv = layer_backward(
        grad_first, first_saved, weights_p, vect_p, my_len, 1, trees, launch_p
    )
    grad_rows = grad_inputs.astype(BF)

    def gathered_up(turn):
        spot = my_slots - turn * room
        here = (spot >= 0) & (spot < room)
        place = jnp.where(here, my_owners * room + spot, -1)
        chosen = lax.broadcasted_iota(jnp.int32, (count * room, seq_len), 0) == place[None, :]
        return dot_plain(chosen.astype(BF), grad_rows).astype(BF)

    def settle(sought, got, total_rows):
        landing = (
            lax.broadcasted_iota(jnp.int32, (slice_rows, count * room), 0) == sought[None, :]
        )
        return total_rows + dot_plain(landing.astype(BF), got)

    def give(turn, total_rows):
        got = lax.all_to_all(gathered_up(turn), every, 0, 0, tiled=True)
        return settle(asked(turn), got, total_rows)

    sent_back = gathered_up(0)

    middle = part_qkv.shape[1] // 2
    sides = grad_vect_p.reshape(2, -1, D)
    keep = lax.dynamic_index_in_dim(sides, at_core, 0, False)
    keep = keep + across(lax.dynamic_index_in_dim(sides, 1 - at_core, 0, False), "core")
    keep = keep.astype(BF).reshape(block, 1, -1)
    width_p = keep.shape[2]
    keep = jnp.pad(keep, ((0, 0), (0, 15), (0, middle - width_p)))
    qkv_one = part_qkv[:, :middle].reshape(block, -1, middle)
    height = qkv_one.shape[1]
    qkv_one = jnp.concatenate([qkv_one, keep], 1).reshape(-1, middle)
    tree_one = Reduce(qkv_one, rest, rest[::-1], unswap)
    tree_two = Reduce(part_qkv[:, middle:], rest, rest, unswap)
    trees += [tree_one, tree_two]
    got_back = lax.all_to_all(sent_back, every, 0, 0, tiled=True)

    posit_tree = Reduce(grad_rows, posit_names, ("core",) + shard_names[::-1])
    posit_tree.step()
    (got_back,) = meet([got_back], trees + [posit_tree])
    meet([], [tree_one, tree_two, posit_tree])
    grad_table = settle(asked_first, got_back, 0.0)
    grad_posit = posit_tree.result()
    grad_posit = grad_posit + across(grad_posit.astype(BF), "pair").astype(F32)
    grad_posit = jnp.where(at_pair == 0, grad_posit, 0.0)
    grad_vect_sh = jnp.sum(vector_tree.result().reshape(count, -1), 0)[:width_s]
    head_own = head_tree.result()[:slice_rows]
    g_down_s, g_wide_s = shared_trees["down"].result(), shared_trees["qkv"].result()
    g_down_p, g_fore_p = [private_trees[kind][0].result() for kind in ("down", "fore")]
    g_qkv_p, g_qkv_q = tree_one.result(), tree_two.result()
    g_qkv_p, grad_vect_ph = g_qkv_p[:height], g_qkv_p[height, :width_p]
    g_wide_p = jnp.concatenate([g_qkv_p, g_qkv_q, g_fore_p[:, FF:], g_fore_p[:, :FF]], 1)

    grad_table = grad_table + head_own
    grad_table = lax.fori_loop(1, rounds, give, grad_table)

    all_grads = [
        grad_table,
        grad_posit,
        g_wide_s,
        g_down_s,
        grad_vect_sh,
        g_wide_p[None],
        g_down_p[None],
        grad_vect_ph[None],
    ]
    squares = jnp.zeros((), jnp.float32)
    for gradient in all_grads:
        squares = squares + jnp.sum(gradient * gradient)
    client_at = jnp.arange(clients, dtype=jnp.int32)
    loss_vector = jnp.where(client_at == 2 * at_pair + at_half, own_terms, 0.0)
    figures = jnp.concatenate([squares[None], loss_vector])
    figures = jnp.pad(figures, (0, 127 - clients)).reshape(1, 1, 128)
    figures = jnp.broadcast_to(figures, (count, 1, 128))
    figures = jnp.sum(lax.all_to_all(figures, every, 0, 0, tiled=True)[:, 0], 0)
    grad_norm = jnp.sqrt(figures[0])
    own_client = client_at == 2 * at_pair + at_core
    loss_sum = jnp.sum(jnp.where(own_client, figures[1 : 1 + clients], 0.0))
    count_sum = jnp.sum(jnp.where(own_client, counts_all, 0.0))
    factor = jnp.minimum(1.0, CLIP_NORM / grad_norm)
    g_table, g_posit, g_wide_s, g_down_s, g_vect_s, g_wide_p, g_down_p, g_vect_p = [
        member * factor for member in all_grads
    ]
    results = []
    for state, gradient, rate, decay in (
        ((embedding, embedding_first, embedding_second), g_table, RATE_MATRIX, DECAY),
        ((position_table, position_first, position_second), g_posit, RATE_MATRIX, DECAY),
        ((shared_wide, shared_wide_first, shared_wide_second), g_wide_s, RATE_MATRIX, DECAY),
        ((shared_down, shared_down_first, shared_down_second), g_down_s, RATE_MATRIX, DECAY),
        ((shared_vectors, shared_vectors_first, shared_vectors_second), g_vect_s, RATE_VECTOR, 0.0),
        ((private_wide, private_wide_first, private_wide_second), g_wide_p, RATE_MATRIX, DECAY),
        ((private_down, private_down_first, private_down_second), g_down_p, RATE_MATRIX, DECAY),
        (
            (private_vectors, private_vectors_first, private_vectors_second),
            g_vect_p,
            RATE_VECTOR,
            0.0,
        ),
    ):
        results += adamw(*state, gradient, rate, decay)
    return (*results, loss_sum.reshape(1), count_sum.reshape(1), grad_norm)


def solution(mesh):
    clients, shards = mesh.shape["client"], mesh.shape["shard"]
    depth = shards.bit_length() - 1
    if clients != 4 or shards != 2**depth:
        raise ValueError("mesh sizes")
    shard_names = tuple("s%d" % place for place in range(depth))
    fine = Mesh(
        mesh.devices.reshape((clients // 2, 2) + (2,) * depth), ("pair", "core") + shard_names
    )
    client, shard, both = ("pair", "core"), shard_names, ("pair", "core") + shard_names
    table, block, vector, lot = P(both, None), P(client, shard, None), P(both), P(client, shard)
    in_specs = (
        (block, lot, block, P())
        + (table,) * 12
        + (vector,) * 3
        + (block,) * 6
        + (lot,) * 3
    )
    out_specs = (
        (table,) * 12 + (vector,) * 3 + (block,) * 6 + (lot,) * 3 + (P(client), P(client), P())
    )

    def run(*arrays):
        return per_device(shard_names, *arrays)

    return jax.shard_map(
        run, mesh=fine, in_specs=in_specs, out_specs=out_specs, check_vma=False
    )
```

```python
import jax
import jax.numpy as jnp
from jax import lax
from jax.experimental import pallas as pl
from jax.experimental.pallas import tpu as pltpu
from jax.sharding import Mesh
from jax.sharding import PartitionSpec as P

HD = 64
D = 768
FF = 3072
NPOS = 1024
STEP = 5


SCALE = 0.125
CLIP_NORM = 0.01
RATE_MATRIX = 0.03
RATE_VECTOR = 0.5
DECAY = 0.01
EPSILON = 1e-08
BF = jnp.bfloat16
F32 = jnp.float32
NT = (((1,), (1,)), ((), ()))
TN = (((0,), (0,)), ((), ()))


def dot_plain(former, latter):
    return jnp.dot(former, latter, preferred_element_type=jnp.float32)


def dot_inner(former, latter):
    return lax.dot_general(
        former, latter, (((0,), (0,)), ((), ())), preferred_element_type=jnp.float32
    )


def dot_outer(former, latter):
    return lax.dot_general(
        former, latter, (((1,), (1,)), ((), ())), preferred_element_type=jnp.float32
    )


def layer_norm(values, scales, shifts):
    centre = values - jnp.mean(values, -1, keepdims=True)
    spread = jnp.mean(centre * centre, -1, keepdims=True)
    return centre * lax.rsqrt(spread + 1e-05) * scales + shifts


def gelu_tanh(values):
    return jax.nn.gelu(values, approximate=True)


def split_vectors(vectors, breadth, hidden):
    starts = [
        0,
        breadth,
        2 * breadth,
        3 * breadth,
        4 * breadth,
        5 * breadth,
        6 * breadth,
        7 * breadth,
        7 * breadth + hidden,
        8 * breadth + hidden,
    ]
    return [vectors[starts[position] : starts[position + 1]] for position in range(9)]


def product(former, latter, form):
    return lax.dot_general(former, latter, form, preferred_element_type=F32)


def write_mask(live_ref, mask_ref):
    keys = lax.broadcasted_iota(jnp.int32, mask_ref.shape, 0)
    queries = lax.broadcasted_iota(jnp.int32, mask_ref.shape, 1)
    allowed = (keys <= queries) & (keys < live_ref[0])
    mask_ref[...] = jnp.where(allowed, 0.0, -1e30)


def attend_kernel(live_ref, q_ref, k_ref, v_ref, out_ref, log_ref, mask_ref):
    @pl.when(pl.program_id(0) == 0)
    def _():
        write_mask(live_ref, mask_ref)

    tokens, width = q_ref.shape
    tile = tokens // 2
    for head in range(width // HD):
        cols = slice(head * HD, (head + 1) * HD)
        queries, keys, values = q_ref[:, cols] * SCALE, k_ref[:, cols], v_ref[:, cols]
        for part in range(2):
            begin, end = part * tile, (part + 1) * tile
            scores = product(keys[:end], queries[begin:end], NT) + mask_ref[:end, begin:end]
            highest = jnp.max(scores, 0, keepdims=True)
            exponent = jnp.exp(scores - highest)
            total = jnp.sum(exponent, 0, keepdims=True)
            probs = (exponent * (1.0 / total)).astype(BF)
            mixed = product(values[:end], probs, TN)
            out_ref[begin:end, cols] = mixed.T.astype(BF)
            log_ref[0, head : head + 1, begin:end] = highest + jnp.log(total)


def attend_back_kernel(live_ref, q_ref, k_ref, v_ref, grad_ref, log_ref, out_ref, mask_ref):
    @pl.when(pl.program_id(0) == 0)
    def _():
        write_mask(live_ref, mask_ref)

    tokens, width = q_ref.shape
    tile = tokens // 2
    breadth = out_ref.shape[1] // 3
    sides = [[], [], []]
    for head in range(width // HD):
        cols = slice(head * HD, (head + 1) * HD)
        queries, keys, values = q_ref[:, cols] * SCALE, k_ref[:, cols], v_ref[:, cols]
        grads = grad_ref[:, cols]
        grad_queries, grad_keys, grad_values = [], [], []
        for part in range(2):
            begin, end = part * tile, (part + 1) * tile
            scores = product(keys[:end], queries[begin:end], NT) + mask_ref[:end, begin:end]
            probs = jnp.exp(scores - log_ref[0, head : head + 1, begin:end])
            grad_out = grads[begin:end]
            grad_values.append(
                jnp.dot(probs.astype(BF), grad_out, preferred_element_type=F32)
            )
            grad_probs = product(values[:end], grad_out, NT)
            inner = jnp.sum(grad_probs * probs, 0, keepdims=True)
            grad_scores = (probs * (grad_probs - inner)).astype(BF)
            grad_keys.append(
                jnp.dot(grad_scores, queries[begin:end], preferred_element_type=F32)
            )
            grad_queries.append(product(keys[:end], grad_scores, TN).T * SCALE)
        for side, parts in ((1, grad_keys), (2, grad_values)):
            sides[side].append(
                jnp.concatenate([parts[0] + parts[1][:tile], parts[1][tile:]], 0)
            )
        sides[0].append(jnp.concatenate(grad_queries, 0))
    place = pl.program_id(0) * width
    for side in range(3):
        start = pl.multiple_of(side * breadth + place, width)
        out_ref[:, pl.ds(start, width)] = jnp.concatenate(sides[side], 1).astype(BF)


def attend(joined, live_len):
    tokens, breadth = joined.shape[0], joined.shape[1] // 3
    width = 2 * HD
    pairs = breadth // width
    parts = [
        pl.BlockSpec((tokens, width), lambda i, n, side=side: (0, side * pairs + i))
        for side in range(3)
    ]
    return pl.pallas_call(
        attend_kernel,
        grid_spec=pltpu.PrefetchScalarGridSpec(
            num_scalar_prefetch=1,
            grid=(pairs,),
            in_specs=parts,
            out_specs=[
                pl.BlockSpec((tokens, width), lambda i, n: (0, i)),
                pl.BlockSpec((1, 2, tokens), lambda i, n: (i, 0, 0)),
            ],
            scratch_shapes=[pltpu.VMEM((tokens, tokens), F32)],
        ),
        out_shape=[
            jax.ShapeDtypeStruct((tokens, breadth), BF),
            jax.ShapeDtypeStruct((pairs, 2, tokens), F32),
        ],
        compiler_params=pltpu.CompilerParams(vmem_limit_bytes=32 << 20),
        cost_estimate=pl.CostEstimate(flops=0, bytes_accessed=0, transcendentals=0),
    )(live_len.reshape(1), joined, joined, joined)


def attend_back(joined, log_total, grad_mixed, live_len):
    tokens, breadth = grad_mixed.shape
    width = 2 * HD
    pairs = breadth // width
    parts = [
        pl.BlockSpec((tokens, width), lambda i, n, side=side: (0, side * pairs + i))
        for side in range(3)
    ]
    return pl.pallas_call(
        attend_back_kernel,
        grid_spec=pltpu.PrefetchScalarGridSpec(
            num_scalar_prefetch=1,
            grid=(pairs,),
            in_specs=parts
            + [
                pl.BlockSpec((tokens, width), lambda i, n: (0, i)),
                pl.BlockSpec((1, 2, tokens), lambda i, n: (i, 0, 0)),
            ],
            out_specs=pl.BlockSpec((tokens, 3 * breadth), lambda i, n: (0, 0)),
            scratch_shapes=[pltpu.VMEM((tokens, tokens), F32)],
        ),
        out_shape=jax.ShapeDtypeStruct((tokens, 3 * breadth), BF),
        compiler_params=pltpu.CompilerParams(vmem_limit_bytes=32 << 20),
        cost_estimate=pl.CostEstimate(flops=0, bytes_accessed=0, transcendentals=0),
    )(live_len.reshape(1), joined, joined, joined, grad_mixed, log_total)


def fence(*arrays):
    return lax.optimization_barrier(arrays)


class Tree:
    def tied(self):
        return [self.held] if self.other is None else [self.held, self.other]

    def retie(self, arrays):
        self.held = arrays[0]
        if self.other is not None:
            self.other = arrays[1]

    def step(self):
        if self.other is None:
            self.send()
        else:
            self.advance()

    def result(self):
        while self.open:
            self.step()
        return self.final()


class Gather(Tree):
    def __init__(self, block, names, order, waits=(), lazy=False):
        self.names, self.order, self.rows, self.waits = names, list(order), block.shape, list(waits)
        self.held = block.reshape((1,) * len(names) + block.shape)
        self.other = None
        if not lazy:
            self.send()

    def send(self):
        self.other = across(self.held, self.order[0])

    def advance(self):
        name = self.order.pop(0)
        dim, low_side = self.names.index(name), lax.axis_index(name) == 0
        self.held = jnp.where(
            low_side,
            jnp.concatenate([self.held, self.other], dim),
            jnp.concatenate([self.other, self.held], dim),
        )
        self.other = None
        if self.order:
            self.send()

    @property
    def open(self):
        return bool(self.order)

    def final(self):
        return self.held.reshape((-1,) + self.rows[1:])


class Reduce(Tree):
    def __init__(self, blocks, names, order, after=None, waits=(), lazy=False):
        self.names, self.order, self.after, self.waits = names, list(order), after, list(waits)
        self.tail = blocks.shape[1:]
        self.held = blocks.reshape((2,) * len(names) + (-1,) + self.tail)
        self.other = None
        if not lazy:
            self.send()

    def send(self):
        if self.order:
            name = self.order[0]
            dim, side = self.names.index(name), lax.axis_index(name)
            self.other = across(lax.dynamic_index_in_dim(self.held, 1 - side, dim, True), name)
            self.held = lax.dynamic_index_in_dim(self.held, side, dim, True)
        else:
            self.held = self.held.astype(BF)
            self.other = self.after[0](self.held)

    def advance(self):
        if self.order:
            self.order.pop(0)
            total = self.held.astype(F32) + self.other.astype(F32)
            self.held = total.astype(BF) if self.order else total
        else:
            self.held = self.after[1](self.held, self.other)
            self.after = None
        self.other = None
        if self.open:
            self.send()

    @property
    def open(self):
        return bool(self.order) or self.after is not None

    def final(self):
        return self.held.astype(F32).reshape((-1,) + self.tail)


class Exchange(Tree):
    def __init__(self, packet, names, waits):
        self.held, self.names, self.waits = packet, names, list(waits)
        self.other, self.open = None, True

    def send(self):
        self.other = lax.all_to_all(self.held, self.names, 0, 0, tiled=True)

    def advance(self):
        self.open = False

    def final(self):
        return self.other


def meet(carry, trees):
    due = []
    for tree in trees:
        if tree.open:
            if tree.waits and tree.waits[0] > 0:
                tree.waits[0] -= 1
            else:
                tree.waits = tree.waits[1:]
                due.append(tree)
    flat, spans = list(carry), []
    for tree in due:
        start = len(flat)
        flat += tree.tied()
        spans.append((start, len(flat)))
    flat = fence(*flat)
    for tree, (start, stop) in zip(due, spans):
        tree.retie(flat[start:stop])
        tree.step()
    return flat[: len(carry)]


def core_half(active, lead, side):
    width = active.shape[1] // (2 * lead)
    if width % 128:
        pieces = [
            active[:, (2 * part + core) * width : (2 * part + core + 1) * width]
            for core in range(2)
            for part in range(lead)
        ]
        active, lead, width = jnp.concatenate(pieces, 1), 1, width * lead
    pieces = [
        lax.dynamic_slice_in_dim(active, (2 * part + side) * width, width, 1)
        for part in range(lead)
    ]
    return pieces[0] if lead == 1 else jnp.concatenate(pieces, 1)


def core_reduce(active, grad, lead):
    side = lax.axis_index("core")
    send = dot_inner(core_half(active, lead, 1 - side), grad).astype(BF)
    other = across(send, "core")
    return (dot_inner(core_half(active, lead, side), grad) + other.astype(F32)).astype(BF)


def settled(weight):
    return weight.result() if isinstance(weight, Tree) else weight


def layer_forward(inputs, weights, vectors, live_len, meets):
    breadth = inputs.shape[1]
    parts = split_vectors(vectors, breadth, vectors.shape[0] - 8 * breadth)
    normed = layer_norm(inputs, parts[0], parts[1]).astype(jnp.bfloat16)
    shift_qkv = jnp.concatenate([parts[2], jnp.zeros_like(parts[2]), parts[3]])
    qkvo = settled(weights[0])
    joined = (dot_plain(normed, qkvo[:, : 3 * breadth]) + shift_qkv).astype(jnp.bfloat16)
    mixed_out, log_totals = attend(joined, live_len)
    (mixed_out,) = meet([mixed_out], meets[0])
    middle = inputs + (dot_plain(mixed_out, qkvo[:, 3 * breadth :]) + parts[4])
    normed_two = layer_norm(middle, parts[5], parts[6]).astype(jnp.bfloat16)
    fore = settled(weights[1])
    pre_act = dot_plain(normed_two, fore) + parts[7]
    activ = gelu_tanh(pre_act).astype(jnp.bfloat16)
    (activ,) = meet([activ], meets[1])
    down = settled(weights[2])
    output = middle + (dot_plain(activ, down) + parts[8])
    return (
        output,
        (inputs, normed, joined, mixed_out, log_totals, middle, normed_two, pre_act, activ),
        (qkvo, fore, down),
    )


def layer_backward(grad_out, saved, weights, vectors, live_len, lead, trees, launch):
    inputs, normed, joined, mixed_out, log_totals, middle, normed_two, pre_act, activ = saved
    qkvo, fore, down = weights
    breadth = inputs.shape[1]
    parts = split_vectors(vectors, breadth, down.shape[0])
    grad_y = grad_out.astype(jnp.bfloat16)
    part_down = core_reduce(activ, grad_y, lead)
    grad_act = dot_outer(grad_y, down)
    grad_pre = jax.vjp(gelu_tanh, pre_act)[1](grad_act)[0].astype(jnp.bfloat16)
    grad_pre, part_down = meet([grad_pre, part_down], trees)
    trees.extend(launch("down", part_down))
    part_fore = core_reduce(normed_two, grad_pre, lead)
    grad_norm_two = dot_outer(grad_pre, fore)
    grad_mid_norm, grad_scale_two, grad_shift_two = jax.vjp(layer_norm, middle, parts[5], parts[6])[
        1
    ](grad_norm_two)
    grad_mid = grad_out + grad_mid_norm
    grad_branch = grad_mid.astype(jnp.bfloat16)
    grad_branch, part_fore = meet([grad_branch, part_fore], trees)
    part_proj = core_reduce(mixed_out, grad_branch, lead)
    grad_mixed = dot_outer(grad_branch, qkvo[:, 3 * breadth :]).astype(jnp.bfloat16)
    grad_mixed, part_proj = meet([grad_mixed, part_proj], trees)
    trees.extend(launch("fore", (part_fore, part_proj)))
    grad_joined = attend_back(joined, log_totals, grad_mixed, live_len)
    (grad_joined,) = meet([grad_joined], trees)
    part_qkv = core_reduce(normed, grad_joined, lead)
    grad_normed = dot_outer(grad_joined, qkvo[:, : 3 * breadth])
    (grad_normed,) = meet([grad_normed], trees if lead == 1 else [])
    grad_in_norm, grad_scale_one, grad_shift_one = jax.vjp(layer_norm, inputs, parts[0], parts[1])[
        1
    ](grad_normed)
    grad_in = grad_mid + grad_in_norm
    grad_in, part_qkv = meet([grad_in, part_qkv], trees)
    joined_sums = jnp.sum(grad_joined.astype(jnp.float32), 0)
    rows = [
        grad_scale_one,
        grad_shift_one,
        joined_sums[:breadth],
        joined_sums[2 * breadth :],
        jnp.sum(grad_branch.astype(jnp.float32), 0),
        grad_scale_two,
        grad_shift_two,
        jnp.sum(grad_pre.astype(jnp.float32), 0),
        jnp.sum(grad_y.astype(jnp.float32), 0),
    ]
    grad_vectors = jnp.concatenate([row.reshape(-1, breadth) for row in rows], 0)
    return (grad_in, grad_vectors, part_qkv)


def adamw(weight, first, second, gradient, rate, decay):
    first_new = 0.5 * first + 0.5 * gradient
    second_new = 0.5 * second + 0.5 * gradient * gradient
    first_hat = first_new / (1.0 - 0.5**STEP)
    second_hat = second_new / (1.0 - 0.5**STEP)
    weight_new = weight - rate * (first_hat / (jnp.sqrt(second_hat) + EPSILON) + decay * weight)
    return (weight_new, first_new, second_new)


FLIP = [(0, 1), (1, 0)]


def across(x, name):
    return lax.ppermute(x, name, FLIP)


def per_device(
    shard_names,
    token_ids,
    lengths,
    picked,
    joining,
    embedding,
    embedding_first,
    embedding_second,
    position_table,
    position_first,
    position_second,
    shared_wide,
    shared_wide_first,
    shared_wide_second,
    shared_down,
    shared_down_first,
    shared_down_second,
    shared_vectors,
    shared_vectors_first,
    shared_vectors_second,
    private_wide,
    private_wide_first,
    private_wide_second,
    private_down,
    private_down_first,
    private_down_second,
    private_vectors,
    private_vectors_first,
    private_vectors_second,
):
    half, rest = shard_names[0], shard_names[1:]
    every = ("pair", "core") + shard_names
    crew = ("core",) + rest
    shards = 2 ** len(shard_names)
    clients = 4
    count = clients * shards
    at_pair, at_core, at_half = (lax.axis_index(n) for n in ("pair", "core", half))
    device_at = lax.axis_index(every)
    shard_at = lax.axis_index(shard_names)
    swap_pairs = []
    block = shards // 2
    for pair in range(clients // 2):
        for spot in range(block):
            former = ((pair * 2 + 0) * 2 + 1) * block + spot
            latter = ((pair * 2 + 1) * 2 + 0) * block + spot
            swap_pairs += [(former, latter), (latter, former)]

    seq_len = token_ids.shape[2]
    picks = picked.shape[2]
    slice_rows = embedding.shape[0]

    wide_b = private_wide[0].astype(BF)
    down_b = private_down[0].astype(BF)
    shared_b = shared_wide.astype(BF)
    shared_down_b = shared_down.astype(BF)
    cut = 4 * D

    ids = token_ids[0, 0]
    same = ids[:, None] == ids[None, :]
    at_row = lax.broadcasted_iota(jnp.int32, (seq_len, seq_len), 0)
    at_col = lax.broadcasted_iota(jnp.int32, (seq_len, seq_len), 1)
    first_at = jnp.min(jnp.where(same, at_col, seq_len), 1)
    is_first = first_at == jnp.arange(seq_len, dtype=jnp.int32)
    owners = ids // slice_rows
    slot = jnp.sum(
        (
            (owners[:, None] == owners[None, :]) & is_first[None, :] & (at_col < first_at[:, None])
        ).astype(jnp.int32),
        1,
    )

    vect_own = [shared_vectors, private_vectors[0]]
    pieces = [
        ids.astype(F32),
        slot.astype(F32),
        is_first.astype(F32),
        picked[0, 0].astype(F32),
        lengths[0].astype(F32),
    ] + [v.astype(BF).astype(F32) for v in vect_own]
    starts = [0]
    for piece in pieces:
        starts.append(starts[-1] + piece.shape[0])
    room = max(16, 1024 // count)
    owner_at = jnp.arange(count, dtype=jnp.int32)[:, None, None]
    room_at = jnp.arange(room, dtype=jnp.int32)[None, :, None]
    sought = (owners == owner_at) & (jnp.where(is_first, slot, -1) == room_at)
    sought = jnp.sum(jnp.where(sought, ids - owner_at * slice_rows, 0), 2).astype(F32)
    message = jnp.concatenate(pieces)
    message = jnp.broadcast_to(message, (count,) + message.shape)
    message = jnp.concatenate([message, sought], 1)
    width = message.shape[1]
    message = jnp.pad(message, ((0, 0), (0, -width % 1024))).reshape(count, -1, 128)
    first_moved = lax.ppermute(wide_b[:, :cut], every, swap_pairs)
    table_own = embedding.astype(BF)
    pad_rows = -(-slice_rows // 16) * 16
    table_four = Gather(
        jnp.pad(table_own, ((0, pad_rows - slice_rows), (0, 0))),
        ("pair", "core"),
        ("pair", "core"),
    )
    def moved(x):
        return lax.ppermute(x, every, swap_pairs)

    board = lax.all_to_all(message, every, 0, 0, tiled=True).reshape(count, -1)
    posit_b = lax.all_gather(position_table.astype(BF), every, axis=0, tiled=True)[:seq_len]
    posit_names = ("core",) + shard_names
    spread = shard_names + ("pair", "core")
    shared_one = Gather(shared_b[:, :cut], every, spread)
    board, wide_b, down_b, shared_b, shared_down_b = fence(
        board, wide_b, down_b, shared_b, shared_down_b
    )
    (board, first_moved) = meet([board, first_moved], [shared_one])
    stays = at_core == at_half
    there, back = rest + ("core",), rest[::-1] + ("core",)
    private_one = Gather(jnp.where(stays, wide_b[:, :cut], first_moved), crew, back)
    second_moved, third_moved = moved(wide_b[:, cut:]), moved(down_b)

    filled = jnp.where(
        jnp.arange(clients * pad_rows, dtype=jnp.int32) % pad_rows < slice_rows, 0.0, -jnp.inf
    )

    def posted(place):
        return board[:, starts[place] : starts[place + 1]]

    def hosted(x):
        x = x.reshape((clients // 2, 2, 2, block) + x.shape[1:])
        return jnp.swapaxes(x, 1, 2).reshape((count,) + x.shape[4:])

    all_ids, all_slots, all_first, all_picks, all_lens = [
        hosted(posted(place).astype(jnp.int32)) for place in range(5)
    ]
    vect_s = posted(5).reshape(-1)
    vect_p = lax.dynamic_index_in_dim(
        posted(6).reshape(clients, -1), 2 * at_pair + at_half, 0, False
    )

    all_live = all_picks < all_lens - 1
    live_counts = jnp.sum(all_live.astype(F32), 1).reshape(clients // 2, 2, 2, block)
    counts_all = jnp.sum(live_counts, (1, 3)).reshape(-1)
    joining_f = joining.astype(F32)
    share_all = joining_f / (jnp.sum(joining_f) * counts_all)

    my_ids = lax.dynamic_index_in_dim(all_ids, device_at, 0, False)
    my_slots = lax.dynamic_index_in_dim(all_slots, device_at, 0, False)
    my_picks = lax.dynamic_index_in_dim(all_picks, device_at, 0, False)
    my_len = lax.dynamic_index_in_dim(all_lens, device_at, 0, False)[0]
    my_owners = my_ids // slice_rows

    rounds = jnp.max(all_slots) // room + 1
    in_slice = all_ids - device_at * slice_rows
    wanted = (all_first > 0) & (in_slice >= 0) & (in_slice < slice_rows)

    def asked(turn):
        spots = turn * room + jnp.arange(room, dtype=jnp.int32)
        hits = wanted[:, None, :] & (all_slots[:, None, :] == spots[None, :, None])
        return jnp.sum(jnp.where(hits, in_slice[:, None, :], 0), 2).reshape(-1)

    asked_first = hosted(board[:, width - room : width].astype(jnp.int32)).reshape(-1)

    def land(turn, rows, got):
        spot = my_slots - turn * room
        here = (spot >= 0) & (spot < room)
        found = jnp.take(got, jnp.where(here, my_owners * room + spot, 0), axis=0, mode="clip")
        return jnp.where(here[:, None], found, rows)

    def fetch(turn, rows):
        sent = jnp.take(table_own, asked(turn), axis=0, mode="clip")
        return land(turn, rows, lax.all_to_all(sent, every, 0, 0, tiled=True))

    sent = jnp.take(table_own, asked_first, axis=0, mode="clip")
    got = lax.all_to_all(sent, every, 0, 0, tiled=True)
    shared_two = Gather(shared_b[:, cut:], every, spread)
    shared_three = Gather(shared_down_b, every, spread)
    second_moved, third_moved = meet([second_moved, third_moved], [private_one, shared_one])
    private_two = Gather(jnp.where(stays, wide_b[:, cut:], second_moved), crew, back)
    private_three = Gather(jnp.where(stays, down_b, third_moved), crew, there)
    meet([], [shared_one])
    meet([], [private_one, private_two, private_three, shared_two, shared_three])
    meet([], [shared_two, shared_three])
    (got,) = meet([got], [table_four])
    rows = land(0, jnp.zeros((seq_len, D), BF), got)
    rows = lax.fori_loop(1, rounds, fetch, rows)
    inputs = rows.astype(F32) + posit_b.astype(F32)

    weights_p = (private_one, private_two, private_three)
    weights_s = (shared_one, shared_two, shared_three)
    first_out, first_saved, weights_p = layer_forward(
        inputs, weights_p, vect_p, my_len, ([private_two, private_three, shared_one, shared_two], [shared_three])
    )
    second_out, second_saved, weights_s = layer_forward(
        first_out, weights_s, vect_s[: 8 * D + FF], my_len, ([shared_two, shared_three], [])
    )

    final_scale = vect_s[8 * D + FF : 9 * D + FF]
    final_shift = vect_s[9 * D + FF : 10 * D + FF]
    final_in = jnp.take(second_out, my_picks, axis=0, mode="clip")
    final_b = layer_norm(final_in, final_scale, final_shift).astype(BF)
    target_rows = jnp.take(rows, my_picks + 1, axis=0, mode="clip").astype(F32)

    scored_tree = Gather(final_b, shard_names, shard_names)
    meet([final_b], [scored_tree])
    table_four = table_four.result()
    scored = scored_tree.result()

    def group(x):
        x = x.reshape((clients, shards) + x.shape[1:])
        return lax.dynamic_index_in_dim(x, 2 * at_pair + at_core, 0, False)

    group_ids, group_picks, group_live = group(all_ids), group(all_picks), group(all_live)
    seq_at = lax.broadcasted_iota(jnp.int32, (shards, picks, seq_len), 2)
    targets = jnp.sum(
        jnp.where(seq_at == group_picks[:, :, None] + 1, group_ids[:, None, :], 0), 2
    ).reshape(-1)
    host_clients = 2 * at_pair + jnp.arange(shards, dtype=jnp.int32) // block
    weight = jnp.where(group_live, jnp.take(share_all, host_clients)[:, None], 0.0).reshape(-1)
    target_owner = targets // slice_rows
    local_target = jnp.where(
        target_owner % shards == shard_at,
        target_owner // shards * pad_rows + targets % slice_rows,
        -1,
    )
    logits = dot_outer(scored, table_four) + filled
    hit = lax.broadcasted_iota(jnp.int32, logits.shape, 1) == local_target[:, None]
    part_max = jnp.max(logits, -1)
    exponent = jnp.exp(logits - part_max[:, None])
    part_sum = jnp.sum(exponent, -1)
    part_target = jnp.sum(jnp.where(hit, logits, 0.0), -1)
    exponent, part_sum, part_target = fence(exponent.astype(BF), part_sum, part_target)
    pulled = dot_plain(exponent, table_four)
    stats = jnp.stack([part_max, part_sum, part_target])
    stats = lax.all_to_all(
        jnp.broadcast_to(stats, (shards,) + stats.shape), shard_names, 0, 0, tiled=True
    )
    pulled, stats = fence(pulled, stats)
    top = jnp.max(stats[:, 0], 0)
    total = jnp.sum(stats[:, 1] * jnp.exp(stats[:, 0] - top), 0)
    target_logit = jnp.sum(stats[:, 2], 0)
    log_all = top + jnp.log(total)
    pulled = (pulled * (weight * jnp.exp(part_max - log_all))[:, None]).astype(BF)
    pulled_tree = Reduce(pulled, shard_names, shard_names[::-1])
    grad_logits = (
        exponent.astype(F32) * (weight * jnp.exp(part_max - log_all))[:, None]
        - jnp.where(hit, weight[:, None], 0.0)
    ).astype(BF)
    head_parts = []
    for part in jnp.split(grad_logits, clients // 2, 1):
        part = dot_inner(part, scored).astype(BF)
        head_parts += meet([part], [pulled_tree])
    pulled_own = pulled_tree.result()

    def own_rows(x):
        return lax.dynamic_slice_in_dim(x, shard_at * picks, picks, 0)

    own_weight = own_rows(weight)
    grad_final_b = pulled_own - own_weight[:, None] * target_rows
    own_live = lax.dynamic_index_in_dim(group_live, shard_at, 0, False)
    own_terms = jnp.sum(jnp.where(own_live, own_rows(log_all - target_logit), 0.0))
    head_trees = [Reduce(part, ("core",), ("core",), None, (1,)) for part in head_parts]

    grad_final_in, grad_fscale, grad_fshift = jax.vjp(
        layer_norm, final_in, final_scale, final_shift
    )[1](grad_final_b)
    grad_second = jnp.zeros_like(second_out).at[my_picks].add(grad_final_in)
    shared_rest = ("pair",) + shard_names

    def launch_s(kind, part):
        if kind == "fore":
            shared_trees[kind] = part
            return []
        if kind == "qkv":
            part = jnp.concatenate([part, *shared_trees["fore"][::-1]], 1)
        waits = (2,) if kind == "down" else (3, 1)
        shared_trees[kind] = Reduce(
            part, shared_rest, ("pair",) + shard_names[::-1], None, waits
        )
        return [shared_trees[kind]]

    unswap = (
        lambda x: lax.ppermute(x, every, swap_pairs),
        lambda x, other: jnp.where(at_core == at_half, x, other),
    )
    waits_p = {"down": (2,), "fore": (1,)}

    def launch_p(kind, part):
        order = rest[::-1] if kind == "down" else rest
        if kind == "fore":
            part = jnp.concatenate(part, 1)
        private_trees[kind] = [Reduce(part, rest, order, unswap, waits_p[kind])]
        return private_trees[kind]

    shared_trees, private_trees, trees = {}, {}, list(head_trees)
    grad_first, grad_vect_s, part_qkv = layer_backward(
        grad_second,
        second_saved,
        weights_s,
        vect_s[: 8 * D + FF],
        my_len,
        clients // 2,
        trees,
        launch_s,
    )
    trees.extend(launch_s("qkv", part_qkv))
    head_tree = Reduce(
        jnp.concatenate([tree.result().astype(BF) for tree in head_trees], 0),
        ("pair",),
        ("pair",),
        None,
        (3, 2),
        True,
    )
    trees.append(head_tree)
    vector_s = jnp.concatenate([grad_vect_s, grad_fscale[None], grad_fshift[None]], 0)
    vector_s = vector_s.reshape(count, -1)
    width_s = vector_s.shape[1]
    vector_s = jnp.pad(vector_s, ((0, 0), (0, -width_s % 1024))).reshape(count, -1, 128)
    vector_tree = Exchange(vector_s, every, (0, 2))
    trees.append(vector_tree)
    grad_inputs, grad_vect_p, part_qkv = layer_backward(
        grad_first, first_saved, weights_p, vect_p, my_len, 1, trees, launch_p
    )
    grad_rows = grad_inputs.astype(BF)

    def gathered_up(turn):
        spot = my_slots - turn * room
        here = (spot >= 0) & (spot < room)
        place = jnp.where(here, my_owners * room + spot, -1)
        chosen = lax.broadcasted_iota(jnp.int32, (count * room, seq_len), 0) == place[None, :]
        return dot_plain(chosen.astype(BF), grad_rows).astype(BF)

    def settle(sought, got, total_rows):
        landing = (
            lax.broadcasted_iota(jnp.int32, (slice_rows, count * room), 0) == sought[None, :]
        )
        return total_rows + dot_plain(landing.astype(BF), got)

    def give(turn, total_rows):
        got = lax.all_to_all(gathered_up(turn), every, 0, 0, tiled=True)
        return settle(asked(turn), got, total_rows)

    sent_back = gathered_up(0)

    middle = part_qkv.shape[1] // 2
    sides = grad_vect_p.reshape(2, -1, D)
    keep = lax.dynamic_index_in_dim(sides, at_core, 0, False)
    keep = keep + across(lax.dynamic_index_in_dim(sides, 1 - at_core, 0, False), "core")
    keep = keep.astype(BF).reshape(block, 1, -1)
    width_p = keep.shape[2]
    keep = jnp.pad(keep, ((0, 0), (0, 15), (0, middle - width_p)))
    qkv_one = part_qkv[:, :middle].reshape(block, -1, middle)
    height = qkv_one.shape[1]
    qkv_one = jnp.concatenate([qkv_one, keep], 1).reshape(-1, middle)
    tree_one = Reduce(qkv_one, rest, rest[::-1], unswap)
    tree_two = Reduce(part_qkv[:, middle:], rest, rest, unswap)
    trees += [tree_one, tree_two]
    got_back = lax.all_to_all(sent_back, every, 0, 0, tiled=True)

    posit_tree = Reduce(grad_rows, posit_names, ("core",) + shard_names[::-1])
    posit_tree.step()
    (got_back,) = meet([got_back], trees + [posit_tree])
    meet([], [tree_one, tree_two, posit_tree])
    grad_table = settle(asked_first, got_back, 0.0)
    grad_posit = posit_tree.result()
    grad_posit = grad_posit + across(grad_posit.astype(BF), "pair").astype(F32)
    grad_posit = jnp.where(at_pair == 0, grad_posit, 0.0)
    grad_vect_sh = jnp.sum(vector_tree.result().reshape(count, -1), 0)[:width_s]
    head_own = head_tree.result()[:slice_rows]
    g_down_s, g_wide_s = shared_trees["down"].result(), shared_trees["qkv"].result()
    g_down_p, g_fore_p = [private_trees[kind][0].result() for kind in ("down", "fore")]
    g_qkv_p, g_qkv_q = tree_one.result(), tree_two.result()
    g_qkv_p, grad_vect_ph = g_qkv_p[:height], g_qkv_p[height, :width_p]
    g_wide_p = jnp.concatenate([g_qkv_p, g_qkv_q, g_fore_p[:, FF:], g_fore_p[:, :FF]], 1)

    grad_table = grad_table + head_own
    grad_table = lax.fori_loop(1, rounds, give, grad_table)

    all_grads = [
        grad_table,
        grad_posit,
        g_wide_s,
        g_down_s,
        grad_vect_sh,
        g_wide_p[None],
        g_down_p[None],
        grad_vect_ph[None],
    ]
    squares = jnp.zeros((), jnp.float32)
    for gradient in all_grads:
        squares = squares + jnp.sum(gradient * gradient)
    client_at = jnp.arange(clients, dtype=jnp.int32)
    loss_vector = jnp.where(client_at == 2 * at_pair + at_half, own_terms, 0.0)
    figures = jnp.concatenate([squares[None], loss_vector])
    figures = jnp.pad(figures, (0, 127 - clients)).reshape(1, 1, 128)
    figures = jnp.broadcast_to(figures, (count, 1, 128))
    figures = jnp.sum(lax.all_to_all(figures, every, 0, 0, tiled=True)[:, 0], 0)
    grad_norm = jnp.sqrt(figures[0])
    own_client = client_at == 2 * at_pair + at_core
    loss_sum = jnp.sum(jnp.where(own_client, figures[1 : 1 + clients], 0.0))
    count_sum = jnp.sum(jnp.where(own_client, counts_all, 0.0))
    factor = jnp.minimum(1.0, CLIP_NORM / grad_norm)
    g_table, g_posit, g_wide_s, g_down_s, g_vect_s, g_wide_p, g_down_p, g_vect_p = [
        member * factor for member in all_grads
    ]
    results = []
    for state, gradient, rate, decay in (
        ((embedding, embedding_first, embedding_second), g_table, RATE_MATRIX, DECAY),
        ((position_table, position_first, position_second), g_posit, RATE_MATRIX, DECAY),
        ((shared_wide, shared_wide_first, shared_wide_second), g_wide_s, RATE_MATRIX, DECAY),
        ((shared_down, shared_down_first, shared_down_second), g_down_s, RATE_MATRIX, DECAY),
        ((shared_vectors, shared_vectors_first, shared_vectors_second), g_vect_s, RATE_VECTOR, 0.0),
        ((private_wide, private_wide_first, private_wide_second), g_wide_p, RATE_MATRIX, DECAY),
        ((private_down, private_down_first, private_down_second), g_down_p, RATE_MATRIX, DECAY),
        (
            (private_vectors, private_vectors_first, private_vectors_second),
            g_vect_p,
            RATE_VECTOR,
            0.0,
        ),
    ):
        results += adamw(*state, gradient, rate, decay)
    return (*results, loss_sum.reshape(1), count_sum.reshape(1), grad_norm)


def solution(mesh):
    clients, shards = mesh.shape["client"], mesh.shape["shard"]
    depth = shards.bit_length() - 1
    if clients != 4 or shards != 2**depth:
        raise ValueError("mesh sizes")
    shard_names = tuple("s%d" % place for place in range(depth))
    fine = Mesh(
        mesh.devices.reshape((clients // 2, 2) + (2,) * depth), ("pair", "core") + shard_names
    )
    client, shard, both = ("pair", "core"), shard_names, ("pair", "core") + shard_names
    table, block, vector, lot = P(both, None), P(client, shard, None), P(both), P(client, shard)
    in_specs = (
        (block, lot, block, P())
        + (table,) * 12
        + (vector,) * 3
        + (block,) * 6
        + (lot,) * 3
    )
    out_specs = (
        (table,) * 12 + (vector,) * 3 + (block,) * 6 + (lot,) * 3 + (P(client), P(client), P())
    )

    def run(*arrays):
        return per_device(shard_names, *arrays)

    return jax.shard_map(
        run, mesh=fine, in_specs=in_specs, out_specs=out_specs, check_vma=False
    )
```
